32 devices in a mesh: batch: 8 (over z, y), tensor: 4 (over x, core).
Axes of the slice: x: 2, y: 2, z: 4, core: 2. Of those that a mesh axis runs over, the one named last changes fastest.
Arguments:
- layer_input: bfloat16 [24576, 768], P(('batch', 'tensor')), may hold values from -6 to 6
- doc_lengths: int32 [8, 4], P('batch'), may hold values from 1 to 2048, 3072 in all within a row
- first_gain: bfloat16 [768], replicated, may hold values from 0.25 to 1.75
- first_shift: bfloat16 [768], replicated, may hold values from -2 to 2
- w_query: bfloat16 [768, 768], P(None, 'tensor'), may hold values from -0.21875 to 0.21875
- w_key: bfloat16 [768, 768], P(None, 'tensor'), may hold values from -0.21875 to 0.21875
- w_value: bfloat16 [768, 768], P(None, 'tensor'), may hold values from -0.21875 to 0.21875
- query_bias: bfloat16 [768], P('tensor'), may hold values from -2 to 2
- value_bias: bfloat16 [768], P('tensor'), may hold values from -2 to 2
- inner_gain: bfloat16 [768], P('tensor'), may hold values from 0.25 to 1.75
- inner_shift: bfloat16 [768], P('tensor'), may hold values from -2 to 2
- w_proj: bfloat16 [768, 768], P('tensor'), may hold values from -0.21875 to 0.21875
- proj_bias: bfloat16 [768], replicated, may hold values from -2 to 2
- second_gain: bfloat16 [768], replicated, may hold values from 0.25 to 1.75
- second_shift: bfloat16 [768], replicated, may hold values from -2 to 2
- w_in: bfloat16 [768, 3072], P(None, 'tensor'), may hold values from -0.21875 to 0.21875
- in_bias: bfloat16 [3072], P('tensor'), may hold values from -2 to 2
- hidden_gain: bfloat16 [3072], P('tensor'), may hold values from 0.25 to 1.75
- hidden_shift: bfloat16 [3072], P('tensor'), may hold values from -2 to 2
- w_out: bfloat16 [3072, 768], P('tensor'), may hold values from -0.109375 to 0.109375
- out_bias: bfloat16 [768], replicated, may hold values from -2 to 2
- cotangent: bfloat16 [24576, 768], P(('batch', 'tensor')), may hold values from -6 to 6
Outputs:
- layer_output: bfloat16 [24576, 768], P(('batch', 'tensor'))
- input_grad: float32 [24576, 768], P(('batch', 'tensor'))
- grad_first_gain: float32 [768], P(('batch', 'tensor'))
- grad_first_shift: float32 [768], P(('batch', 'tensor'))
- grad_w_query: float32 [768, 768], P('batch', 'tensor')
- grad_w_key: float32 [768, 768], P('batch', 'tensor')
- grad_w_value: float32 [768, 768], P('batch', 'tensor')
- grad_query_bias: float32 [768], P(('batch', 'tensor'))
- grad_value_bias: float32 [768], P(('batch', 'tensor'))
- grad_inner_gain: float32 [768], P(('batch', 'tensor'))
- grad_inner_shift: float32 [768], P(('batch', 'tensor'))
- grad_w_proj: float32 [768, 768], P('tensor', 'batch')
- grad_proj_bias: float32 [768], P(('batch', 'tensor'))
- grad_second_gain: float32 [768], P(('batch', 'tensor'))
- grad_second_shift: float32 [768], P(('batch', 'tensor'))
- grad_w_in: float32 [768, 3072], P('batch', 'tensor')
- grad_in_bias: float32 [3072], P(('batch', 'tensor'))
- grad_hidden_gain: float32 [3072], P(('batch', 'tensor'))
- grad_hidden_shift: float32 [3072], P(('batch', 'tensor'))
- grad_w_out: float32 [3072, 768], P('tensor', 'batch')
- grad_out_bias: float32 [768], P(('batch', 'tensor'))
The draws below stay inside these ranges and needn't reach their ends.
Inputs may be any that keep to these rules, and one draw needn't show every extreme that they name: `doc_lengths`: each row's lengths sum to 3072; in every row the longest document has exactly 2048 tokens.
All inputs are finite; a program needn't handle non-finite values.
Results may differ from the reference program's by a relative error of at most 0.02.
Values may be sent and summed in bfloat16 or wider, within the bound.
A program may use at most 256 MiB of HBM per device.

```python
import math
import jax
import jax.numpy as jnp
import numpy as np
from jax import lax

D = 768
HEADS = 12
HDIM = 64
FF = 3072
TOK_DEV = 3072
DOCS = 4
BLK = 512
MAXLEN = 2048
TOKENS = 24576
N_BATCH = 8


def steps_of(stream_key, shape, cuts, least, largest):
    def one(position, parts):
        steps = jax.random.uniform(jax.random.fold_in(jax.random.fold_in(stream_key, 6), position), (parts,), jnp.float32, least / len(cuts), largest / len(cuts))
        return jnp.repeat(jnp.exp(steps), shape[position] // parts).reshape((-1,) + (1,) * (len(shape) - position - 1))

    level = one(*cuts[0])
    for cut in cuts[1:]:
        level = level * one(*cut)
    return level


def split_up(number_of, total, most, lean):
    weights = [(1 << 20) // math.isqrt(grade ** lean) + 1 for grade in range(2, number_of + 1)]
    surplus, given = total - most - (number_of - 1), [1] * (number_of - 1)
    while surplus > 0:
        candidates = [i for i in range(number_of - 1) if given[i] < most]
        mass, remaining = sum([weights[i] for i in candidates]), surplus
        for i in candidates:
            more = min(most - given[i], max(1, remaining * weights[i] // mass), surplus)
            given[i] = given[i] + more
            surplus = surplus - more
    return np.array([most] + given)


def uneven(own_key, count, total, reach, slope):
    if count == 2:
        one = jax.random.randint(own_key, (), max(1, total - reach), min(reach, total - 1) + 1)
        return jnp.stack([one, total - one])
    sizes = jnp.asarray(split_up(count, total, reach, slope), jnp.int32)
    twos = (count - 1) // 2
    donor, sink = sizes[1:1 + 2 * twos:2], sizes[2:2 + 2 * twos:2]
    room = jnp.minimum(donor - 1, reach - sink)
    shifted = jax.random.randint(jax.random.fold_in(own_key, 1), (twos,), 0, 1 << 20) % (room + 1)
    sizes = sizes.at[1:1 + 2 * twos:2].set(donor - shifted).at[2:2 + 2 * twos:2].set(sink + shifted)
    return sizes[jax.random.permutation(jax.random.fold_in(own_key, 2), count)]


def normal_values(key, extent, scale, most, split=(), held_as=jnp.bfloat16):
    drawn = jax.random.normal(key, extent, jnp.float32) * scale
    if len(split) > 0:
        drawn = steps_of(key, extent, split, -0.22, 0.18) * drawn
    return jnp.clip(drawn, min=-most, max=most).astype(held_as)


def setup_inputs(seed: int = 0) -> dict:
    splits = jax.random.split(jax.random.key(seed), 23)
    return {
        "layer_input": normal_values(splits[0], (TOKENS, D), 1.0, 6.0, ((0, 32),)),
        "doc_lengths": jax.vmap(lambda own: uneven(own, DOCS, TOK_DEV, MAXLEN, 2))(jax.random.split(splits[1], N_BATCH)).reshape((N_BATCH, DOCS)).astype(jnp.int32),
        "first_gain": jnp.clip(1.0 + 0.15 * jax.random.normal(splits[2], (D,), jnp.float32), 0.25, 1.75).astype(jnp.bfloat16),
        "first_shift": normal_values(splits[3], (D,), 0.3, 2.0),
        "w_query": normal_values(splits[4], (D, D), D ** -0.5, 0.21875, ((1, 4),)),
        "w_key": normal_values(splits[5], (D, D), D ** -0.5, 0.21875, ((1, 4),)),
        "w_value": normal_values(splits[6], (D, D), D ** -0.5, 0.21875, ((1, 4),)),
        "query_bias": normal_values(splits[7], (D,), 0.3, 2.0, ((0, 4),)),
        "value_bias": normal_values(splits[8], (D,), 0.3, 2.0, ((0, 4),)),
        "inner_gain": jnp.clip(1.0 + 0.15 * jax.random.normal(splits[9], (D,), jnp.float32), 0.25, 1.75).astype(jnp.bfloat16),
        "inner_shift": normal_values(splits[10], (D,), 0.3, 2.0, ((0, 4),)),
        "w_proj": normal_values(splits[11], (D, D), D ** -0.5, 0.21875, ((0, 4),)),
        "proj_bias": normal_values(splits[12], (D,), 0.3, 2.0),
        "second_gain": jnp.clip(1.0 + 0.15 * jax.random.normal(splits[13], (D,), jnp.float32), 0.25, 1.75).astype(jnp.bfloat16),
        "second_shift": normal_values(splits[14], (D,), 0.3, 2.0),
        "w_in": normal_values(splits[15], (D, FF), D ** -0.5, 0.21875, ((1, 4),)),
        "in_bias": normal_values(splits[16], (FF,), 0.3, 2.0, ((0, 4),)),
        "hidden_gain": jnp.clip(1.0 + 0.15 * jax.random.normal(splits[17], (FF,), jnp.float32), 0.25, 1.75).astype(jnp.bfloat16),
        "hidden_shift": normal_values(splits[18], (FF,), 0.3, 2.0, ((0, 4),)),
        "w_out": normal_values(splits[19], (FF, D), FF ** -0.5, 0.109375, ((0, 4),)),
        "out_bias": normal_values(splits[20], (D,), 0.3, 2.0),
        "cotangent": normal_values(splits[21], (TOKENS, D), 1.0, 6.0, ((0, 32),)),
    }


EPS = 1e-05
SCALE = 0.125

@jax.custom_vjp
def low(v):
    return lax.optimization_barrier(v.astype(jnp.bfloat16)).astype(jnp.float32)

@jax.custom_vjp
def low_back(v):
    return v

def low_keep(v):
    return (low(v), None)

def low_pass(kept, grad):
    return (grad,)

def back_keep(v):
    return (v, None)

def back_low(kept, grad):
    return (low(grad),)
low.defvjp(low_keep, low_pass)
low_back.defvjp(back_keep, back_low)

def rounded_both(values):
    return low_back(low(values))

def matmul(left, right):
    return jnp.dot(left, right, precision=lax.Precision.HIGHEST, preferred_element_type=jnp.float32)

def layer_norm(values, gain, shift):
    mean = lax.optimization_barrier(jnp.mean(values, -1, keepdims=True))
    spread = lax.optimization_barrier(jnp.mean(values * values, -1, keepdims=True)) - mean * mean
    return (values - mean) * lax.rsqrt(spread + EPS) * gain + shift

def segment_ids(lengths, total):
    ends = jnp.cumsum(lengths)
    places = jnp.arange(total, dtype=jnp.int32)
    return lax.optimization_barrier(jnp.sum((places[:, None] >= ends[None, :]).astype(jnp.int32), 1))

def group_forward(rows, lengths, weights):
    first_gain, first_shift, w_query, w_key, w_value, query_bias, value_bias, inner_gain, inner_shift, w_proj, proj_bias, second_gain, second_shift, w_in, in_bias, hidden_gain, hidden_shift, w_out, out_bias = weights
    normed = low(layer_norm(rows, first_gain, first_shift))
    queries = rounded_both(matmul(normed, w_query) + query_bias).reshape(TOK_DEV, HEADS, HDIM)
    keys = rounded_both(matmul(normed, w_key)).reshape(TOK_DEV, HEADS, HDIM)
    values = rounded_both(matmul(normed, w_value) + value_bias).reshape(TOK_DEV, HEADS, HDIM)
    segments = segment_ids(lengths, TOK_DEV)

    def attend_block(block):
        first = (block * BLK).astype(jnp.int32)
        query_block = lax.dynamic_slice_in_dim(queries, first, BLK, 0)
        raw = low_back(jnp.einsum('qhd,khd->hqk', query_block, keys, precision=lax.Precision.HIGHEST)) * SCALE
        rows_at = first + jnp.arange(BLK, dtype=jnp.int32)
        cols_at = jnp.arange(TOK_DEV, dtype=jnp.int32)
        seg_block = lax.dynamic_slice_in_dim(segments, first, BLK, 0)
        allowed = (seg_block[:, None] == segments[None, :]) & (cols_at[None, :] <= rows_at[:, None])
        scores = jnp.where(allowed[None], raw, -1e+30)
        probs = low(jax.nn.softmax(scores, -1))
        return jnp.einsum('hqk,khd->qhd', probs, values, precision=lax.Precision.HIGHEST)
    blocks = lax.map(jax.checkpoint(attend_block), jnp.arange(TOK_DEV // BLK, dtype=jnp.int32))
    heads_out = low_back(blocks.reshape(TOK_DEV, D))
    inner = low(layer_norm(heads_out, inner_gain, inner_shift))
    mixed = rows + low_back(matmul(inner, w_proj) + proj_bias)
    second = low(layer_norm(mixed, second_gain, second_shift))
    pre_act = low_back(matmul(second, w_in) + in_bias)
    hidden = low(layer_norm(jax.nn.gelu(pre_act), hidden_gain, hidden_shift))
    return mixed + low_back(matmul(hidden, w_out) + out_bias)

def reference(layer_input, doc_lengths, first_gain, first_shift, w_query, w_key, w_value, query_bias, value_bias, inner_gain, inner_shift, w_proj, proj_bias, second_gain, second_shift, w_in, in_bias, hidden_gain, hidden_shift, w_out, out_bias, cotangent):
    params = tuple((item.astype(jnp.float32) for item in (first_gain, first_shift, w_query, w_key, w_value, query_bias, value_bias, inner_gain, inner_shift, w_proj, proj_bias, second_gain, second_shift, w_in, in_bias, hidden_gain, hidden_shift, w_out, out_bias)))

    def forward(inputs, weights):
        groups = inputs.reshape(N_BATCH, TOK_DEV, D)

        def one_group(pair):
            return group_forward(pair[0], pair[1], weights)
        outputs = lax.map(jax.checkpoint(one_group), (groups, doc_lengths))
        return outputs.reshape(N_BATCH * TOK_DEV, D)
    result, backward = jax.vjp(forward, layer_input.astype(jnp.float32), params)
    input_grad, grads = backward(cotangent.astype(jnp.float32))
    return (result.astype(jnp.bfloat16), input_grad, grads[0], grads[1], grads[2], grads[3], grads[4], grads[5], grads[6], grads[7], grads[8], grads[9], grads[10], grads[11], grads[12], grads[13], grads[14], grads[15], grads[16], grads[17], grads[18])
```

```python
import functools
import math

import jax
import jax.numpy as jnp
from jax import lax
from jax.experimental import pallas as pl
from jax.experimental.pallas import tpu as pltpu
from jax.sharding import PartitionSpec as P

HDIM = 64
EPS = 1e-05
SCALE = 0.125
LOG2E = 1.4426950408889634
NEG = -1e30
F32 = jnp.float32
BF16 = jnp.bfloat16


def dot_nn(a, b):
    return jnp.dot(a, b, preferred_element_type=F32)


def dot_nt(a, b):
    return lax.dot_general(a, b, (((1,), (1,)), ((), ())), preferred_element_type=F32)


def doc_ends(len_ref):
    ends = []
    total = jnp.int32(0)
    for i in range(len_ref.shape[0]):
        total = total + len_ref[i]
        ends.append(total)
    return ends


def doc_start(ends, pos):
    start = jnp.zeros_like(pos)
    for e in ends[:-1]:
        start = jnp.where(pos >= e, e, start)
    return start


def block_ranges(ends, q0, tq, tk):
    first = doc_start(ends, q0)
    last = doc_start(ends, q0 + tq - 1)
    lo = first // tk
    hi = (q0 + tq + tk - 1) // tk
    mid_lo = jnp.minimum((last + tk - 1) // tk, hi)
    mid_hi = jnp.maximum(q0 // tk, mid_lo)
    return lo, mid_lo, mid_hi, hi


def attn_fwd_kernel(tq, tk, nh, len_ref, qkv_ref, out_ref, lse_ref, k_s, v_s):
    step = pl.program_id(0)
    width = nh * HDIM
    total = k_s.shape[1]

    @pl.when(step == 0)
    def _():
        for h in range(nh):
            k_s[h] = qkv_ref[:, width + h * HDIM : width + (h + 1) * HDIM]
            vals = qkv_ref[:, 2 * width + h * HDIM : 2 * width + (h + 1) * HDIM]
            v_s[h, :HDIM, :] = vals.T
            v_s[h, HDIM:, :] = jnp.ones((16, total), BF16)

    q0 = pl.multiple_of(step * tq, tq)
    ends = doc_ends(len_ref)
    lo, mid_lo, mid_hi, hi = block_ranges(ends, q0, tq, tk)
    rows = qkv_ref[pl.ds(q0, tq), 0:width]
    queries = [rows[:, h * HDIM : (h + 1) * HDIM] for h in range(nh)]
    qpos = q0 + lax.broadcasted_iota(jnp.int32, (1, tq), 1)
    qstart = doc_start(ends, qpos)

    def one(masked, kb, carry):
        k0 = pl.multiple_of(kb * tk, tk)
        if masked:
            kpos = k0 + lax.broadcasted_iota(jnp.int32, (tk, tq), 0)
            allowed = (kpos >= qstart) & (kpos <= qpos)
        result = []
        for h in range(nh):
            peak, acc = carry[h]
            s = dot_nt(k_s[h, pl.ds(k0, tk), :], queries[h]) * (SCALE * LOG2E)
            if masked:
                s = jnp.where(allowed, s, NEG)
            new = jnp.maximum(peak, jnp.max(s, 0, keepdims=True))
            p = jnp.exp2(s - new).astype(BF16)
            acc = acc * jnp.exp2(peak - new) + dot_nn(v_s[h, :, pl.ds(k0, tk)], p)
            result.append((new, acc))
        return tuple(result)

    carry = tuple(
        (jnp.full((1, tq), NEG, F32), jnp.zeros((HDIM + 16, tq), F32)) for _ in range(nh)
    )
    carry = lax.fori_loop(lo, mid_lo, functools.partial(one, True), carry)
    carry = lax.fori_loop(mid_lo, mid_hi, functools.partial(one, False), carry)
    carry = lax.fori_loop(mid_hi, hi, functools.partial(one, True), carry)
    outs = []
    for h in range(nh):
        peak, acc = carry[h]
        total_row = acc[HDIM : HDIM + 1]
        outs.append((acc[:HDIM] / total_row).T)
        lse_ref[h : h + 1, :] = peak + jnp.log2(total_row)
    out_ref[...] = jnp.concatenate(outs, 1).astype(BF16)


def attn_fwd(lengths, qkv, tq, tk):
    rows, width3 = qkv.shape
    width = width3 // 3
    nh = width // HDIM
    return pl.pallas_call(
        functools.partial(attn_fwd_kernel, tq, tk, nh),
        out_shape=(
            jax.ShapeDtypeStruct((rows, width), BF16),
            jax.ShapeDtypeStruct((nh, rows), F32),
        ),
        grid_spec=pltpu.PrefetchScalarGridSpec(
            num_scalar_prefetch=1,
            grid=(rows // tq,),
            in_specs=[pl.BlockSpec((rows, width3), lambda i, l: (0, 0))],
            out_specs=(
                pl.BlockSpec((tq, width), lambda i, l: (i, 0)),
                pl.BlockSpec((nh, tq), lambda i, l: (0, i)),
            ),
            scratch_shapes=[
                pltpu.VMEM((nh, rows, HDIM), BF16),
                pltpu.VMEM((nh, HDIM + 16, rows), BF16),
            ],
        ),
        compiler_params=pltpu.CompilerParams(vmem_limit_bytes=48 << 20),
        cost_estimate=pl.CostEstimate(
            flops=2 * 2 * nh * HDIM * rows * rows // 2,
            bytes_accessed=rows * width3 * 2 + rows * width * 2,
            transcendentals=nh * rows * rows // 2,
        ),
        name="attn_fwd",
    )(lengths, qkv)


def attn_bwd_kernel(
    tq, tk, nh, len_ref, qkv_ref, out_ref, grad_ref, lse_ref, dq_ref, dk_ref, dv_ref,
    k_s, kt_s, v_s, dk_s, dv_s,
):
    step = pl.program_id(0)
    width = nh * HDIM
    total = k_s.shape[1]

    @pl.when(step == 0)
    def _():
        for h in range(nh):
            keys = qkv_ref[:, width + h * HDIM : width + (h + 1) * HDIM]
            k_s[h] = keys
            kt_s[h] = keys.T
            v_s[h] = qkv_ref[:, 2 * width + h * HDIM : 2 * width + (h + 1) * HDIM]
        dk_s[...] = jnp.zeros_like(dk_s)
        dv_s[...] = jnp.zeros_like(dv_s)

    q0 = pl.multiple_of(step * tq, tq)
    ends = doc_ends(len_ref)
    lo, mid_lo, mid_hi, hi = block_ranges(ends, q0, tq, tk)
    rows = qkv_ref[pl.ds(q0, tq), 0:width]
    queries = [rows[:, h * HDIM : (h + 1) * HDIM] for h in range(nh)]
    grads = [grad_ref[:, h * HDIM : (h + 1) * HDIM] for h in range(nh)]
    prod = grad_ref[...].astype(F32) * out_ref[...].astype(F32)
    deltas = [
        jnp.sum(prod[:, h * HDIM : (h + 1) * HDIM].T, 0, keepdims=True) for h in range(nh)
    ]
    lses = [lse_ref[h : h + 1, :] for h in range(nh)]
    qpos = q0 + lax.broadcasted_iota(jnp.int32, (1, tq), 1)
    qstart = doc_start(ends, qpos)

    def one(masked, kb, carry):
        k0 = pl.multiple_of(kb * tk, tk)
        if masked:
            kpos = k0 + lax.broadcasted_iota(jnp.int32, (tk, tq), 0)
            allowed = (kpos >= qstart) & (kpos <= qpos)
        result = []
        for h in range(nh):
            s = dot_nt(k_s[h, pl.ds(k0, tk), :], queries[h]) * (SCALE * LOG2E)
            if masked:
                s = jnp.where(allowed, s, NEG)
            p = jnp.exp2(s - lses[h])
            dp = dot_nt(v_s[h, pl.ds(k0, tk), :], grads[h])
            ds = (p * (dp - deltas[h])).astype(BF16)
            dv_s[h, pl.ds(k0, tk), :] += dot_nn(p.astype(BF16), grads[h])
            dk_s[h, pl.ds(k0, tk), :] += dot_nn(ds, queries[h])
            result.append(carry[h] + dot_nn(kt_s[h, :, pl.ds(k0, tk)], ds))
        return tuple(result)

    carry = tuple(jnp.zeros((HDIM, tq), F32) for _ in range(nh))
    carry = lax.fori_loop(lo, mid_lo, functools.partial(one, True), carry)
    carry = lax.fori_loop(mid_lo, mid_hi, functools.partial(one, False), carry)
    carry = lax.fori_loop(mid_hi, hi, functools.partial(one, True), carry)
    dq_ref[...] = (jnp.concatenate([c.T for c in carry], 1) * SCALE).astype(BF16)

    @pl.when(step == pl.num_programs(0) - 1)
    def _():
        dk_ref[...] = (jnp.concatenate([dk_s[h] for h in range(nh)], 1) * SCALE).astype(BF16)
        dv_ref[...] = jnp.concatenate([dv_s[h] for h in range(nh)], 1).astype(BF16)


def attn_bwd(lengths, qkv, out, grad, lse, tq, tk):
    rows, width3 = qkv.shape
    width = width3 // 3
    nh = width // HDIM
    full = jax.ShapeDtypeStruct((rows, width), BF16)
    return pl.pallas_call(
        functools.partial(attn_bwd_kernel, tq, tk, nh),
        out_shape=(full, full, full),
        grid_spec=pltpu.PrefetchScalarGridSpec(
            num_scalar_prefetch=1,
            grid=(rows // tq,),
            in_specs=[
                pl.BlockSpec((rows, width3), lambda i, l: (0, 0)),
                pl.BlockSpec((tq, width), lambda i, l: (i, 0)),
                pl.BlockSpec((tq, width), lambda i, l: (i, 0)),
                pl.BlockSpec((nh, tq), lambda i, l: (0, i)),
            ],
            out_specs=(
                pl.BlockSpec((tq, width), lambda i, l: (i, 0)),
                pl.BlockSpec((rows, width), lambda i, l: (0, 0)),
                pl.BlockSpec((rows, width), lambda i, l: (0, 0)),
            ),
            scratch_shapes=[
                pltpu.VMEM((nh, rows, HDIM), BF16),
                pltpu.VMEM((nh, HDIM, rows), BF16),
                pltpu.VMEM((nh, rows, HDIM), BF16),
                pltpu.VMEM((nh, rows, HDIM), F32),
                pltpu.VMEM((nh, rows, HDIM), F32),
            ],
        ),
        compiler_params=pltpu.CompilerParams(vmem_limit_bytes=56 << 20),
        cost_estimate=pl.CostEstimate(
            flops=5 * 2 * nh * HDIM * rows * rows // 2,
            bytes_accessed=rows * width3 * 4,
            transcendentals=nh * rows * rows // 2,
        ),
        name="attn_bwd",
    )(lengths, qkv, out, grad, lse)


def ln_stats(v, n):
    mean = jnp.sum(v, -1, keepdims=True) * (1.0 / n)
    var = jnp.sum(v * v, -1, keepdims=True) * (1.0 / n) - mean * mean
    return mean, lax.rsqrt(var + EPS)


def ln_back(dh, hat, inv, n):
    m0 = jnp.sum(dh, -1, keepdims=True) * (1.0 / n)
    m1 = jnp.sum(dh * hat, -1, keepdims=True) * (1.0 / n)
    return inv * (dh - m0 - hat * m1)


def col_sum(v):
    return jnp.sum(v, 0, keepdims=True)


def mid_kernel(
    tm, nt, heads_ref, resid_ref, cot_ref, wp_ref, wi_ref, wo_ref, vec_ref, fvec_ref,
    lout_ref, mg_ref, hg_ref, gi_ref, go_ref, gp_ref, vs_ref, fs_ref,
    act_s, dact_s, dh_s, hid_s, pre_s, inner_s, sec_t, cot_t, att_t,
):
    step = pl.program_id(0)
    tiles = pl.num_programs(0) - nt
    width = resid_ref.shape[1]
    ff = nt * wi_ref.shape[2]
    fw = wi_ref.shape[2]
    hw = width // nt

    @pl.when(step == 0)
    def _():
        vs_ref[...] = jnp.zeros_like(vs_ref)
        fs_ref[...] = jnp.zeros_like(fs_ref)

    @pl.when(step < tiles)
    def _():
        r0 = pl.multiple_of(step * tm, tm)
        vec = [vec_ref[i : i + 1, :].astype(F32) for i in range(6)]
        inner_gain, inner_shift, proj_bias, second_gain, second_shift, out_bias = vec
        heads = jnp.concatenate([heads_ref[t] for t in range(nt)], 1).astype(F32)
        mean, inner_inv = ln_stats(heads, width)
        inner_hat = (heads - mean) * inner_inv
        inner_low = (inner_hat * inner_gain + inner_shift).astype(BF16)
        inner_s[pl.ds(r0, tm), :] = inner_low
        mixed = resid_ref[...].astype(F32) + (dot_nn(inner_low, wp_ref[...]) + proj_bias)
        mean, second_inv = ln_stats(mixed, width)
        second_hat = (mixed - mean) * second_inv
        second_low = (second_hat * second_gain + second_shift).astype(BF16)
        sec_t[:, pl.ds(r0, tm)] = second_low.T
        cot_low = cot_ref[...]
        cot_t[:, pl.ds(r0, tm)] = cot_low.T
        cot = cot_low.astype(F32)

        c0 = math.sqrt(2.0 / math.pi)
        c1 = 0.044715
        s0 = jnp.zeros((tm, 1), F32)
        s1 = jnp.zeros((tm, 1), F32)
        for t in range(nt):
            v = dot_nn(second_low, wi_ref[t]) + fvec_ref[t, 0:1, :].astype(F32)
            v2 = v * v
            th = jnp.tanh(v * (c0 + (c0 * c1) * v2))
            half = 0.5 + 0.5 * th
            act = v * half
            dact = half + (0.5 * v) * (1.0 - th * th) * (c0 + (3.0 * c0 * c1) * v2)
            act_s[t] = act
            dact_s[t] = dact
            s0 += jnp.sum(act, -1, keepdims=True)
            s1 += jnp.sum(act * act, -1, keepdims=True)
        mean = s0 * (1.0 / ff)
        inv = lax.rsqrt(s1 * (1.0 / ff) - mean * mean + EPS)
        result = mixed + out_bias
        m0 = jnp.zeros((tm, 1), F32)
        m1 = jnp.zeros((tm, 1), F32)
        for t in range(nt):
            gain = fvec_ref[t, 1:2, :].astype(F32)
            hat = (act_s[t] - mean) * inv
            act_s[t] = hat
            hid = (hat * gain + fvec_ref[t, 2:3, :].astype(F32)).astype(BF16)
            hid_s[t, pl.ds(r0, tm), :] = hid
            result += dot_nn(hid, wo_ref[t])
            gh = dot_nt(cot_low, wo_ref[t])
            gn = gh * hat
            fs_ref[t, 1:2, :] += col_sum(gn)
            fs_ref[t, 2:3, :] += col_sum(gh)
            dh = gh * gain
            dh_s[t] = dh
            m0 += jnp.sum(dh, -1, keepdims=True)
            m1 += jnp.sum(gn * gain, -1, keepdims=True)
        lout_ref[...] = result.astype(BF16)
        m0 = m0 * (1.0 / ff)
        m1 = m1 * (1.0 / ff)
        second_grad = jnp.zeros((tm, width), F32)
        for t in range(nt):
            pre = (inv * (dh_s[t] - m0 - act_s[t] * m1) * dact_s[t]).astype(BF16)
            pre_s[t, pl.ds(r0, tm), :] = pre
            fs_ref[t, 0:1, :] += col_sum(pre.astype(F32))
            second_grad += dot_nt(pre, wi_ref[t])
        vs_ref[3:4, :] += col_sum(second_grad * second_hat)
        vs_ref[4:5, :] += col_sum(second_grad)
        vs_ref[5:6, :] += col_sum(cot)
        mixed_grad = cot + ln_back(second_grad * second_gain, second_hat, second_inv, width)
        mg_ref[...] = mixed_grad
        vs_ref[2:3, :] += col_sum(mixed_grad)
        att = mixed_grad.astype(BF16)
        att_t[:, pl.ds(r0, tm)] = att.T
        grad_inner = dot_nt(att, wp_ref[...])
        vs_ref[0:1, :] += col_sum(grad_inner * inner_hat)
        vs_ref[1:2, :] += col_sum(grad_inner)
        hg = ln_back(grad_inner * inner_gain, inner_hat, inner_inv, width).astype(BF16)
        for t in range(nt):
            hg_ref[t] = hg[:, t * hw : (t + 1) * hw]

    @pl.when(step >= tiles)
    def _():
        t = step - tiles
        gi_ref[0] = dot_nn(sec_t[...], pre_s[t]).astype(BF16)
        go_ref[0] = dot_nn(cot_t[...], hid_s[t]).astype(BF16)

    @pl.when(step == tiles)
    def _():
        gp = dot_nn(att_t[...], inner_s[...]).astype(BF16)
        for t in range(nt):
            gp_ref[t] = gp[:, t * hw : (t + 1) * hw]


def middle(heads, resid, cot, wp, wi, wo, vec, fvec, tm):
    nt, rows, hw = heads.shape
    width = resid.shape[1]
    fw = wi.shape[2]
    tiles = rows // tm
    last = tiles - 1
    tile = lambda i: jnp.minimum(i, last)
    late = lambda i: jnp.maximum(i - tiles, 0)
    once = lambda shape: pl.BlockSpec(
        shape, lambda i: (0,) * len(shape), pipeline_mode=pl.Buffered(1)
    )
    return pl.pallas_call(
        functools.partial(mid_kernel, tm, nt),
        out_shape=(
            jax.ShapeDtypeStruct((rows, width), BF16),
            jax.ShapeDtypeStruct((rows, width), F32),
            jax.ShapeDtypeStruct((nt, rows, hw), BF16),
            jax.ShapeDtypeStruct((nt, width, fw), BF16),
            jax.ShapeDtypeStruct((nt, width, fw), BF16),
            jax.ShapeDtypeStruct((nt, width, hw), BF16),
            jax.ShapeDtypeStruct((8, width), F32),
            jax.ShapeDtypeStruct((nt, 8, fw), F32),
        ),
        grid=(tiles + nt,),
        in_specs=[
            pl.BlockSpec((nt, tm, hw), lambda i: (0, tile(i), 0)),
            pl.BlockSpec((tm, width), lambda i: (tile(i), 0)),
            pl.BlockSpec((tm, width), lambda i: (tile(i), 0)),
            once(wp.shape),
            once(wi.shape),
            once(wo.shape),
            once(vec.shape),
            once(fvec.shape),
        ],
        out_specs=(
            pl.BlockSpec((tm, width), lambda i: (tile(i), 0)),
            pl.BlockSpec((tm, width), lambda i: (tile(i), 0)),
            pl.BlockSpec((nt, tm, hw), lambda i: (0, tile(i), 0)),
            pl.BlockSpec((1, width, fw), lambda i: (late(i), 0, 0)),
            pl.BlockSpec((1, width, fw), lambda i: (late(i), 0, 0)),
            pl.BlockSpec((nt, width, hw), lambda i: (0, 0, 0)),
            pl.BlockSpec((8, width), lambda i: (0, 0)),
            pl.BlockSpec((nt, 8, fw), lambda i: (0, 0, 0)),
        ),
        scratch_shapes=[
            pltpu.VMEM((nt, tm, fw), F32),
            pltpu.VMEM((nt, tm, fw), F32),
            pltpu.VMEM((nt, tm, fw), F32),
            pltpu.VMEM((nt, rows, fw), BF16),
            pltpu.VMEM((nt, rows, fw), BF16),
            pltpu.VMEM((rows, width), BF16),
            pltpu.VMEM((width, rows), BF16),
            pltpu.VMEM((width, rows), BF16),
            pltpu.VMEM((width, rows), BF16),
        ],
        compiler_params=pltpu.CompilerParams(vmem_limit_bytes=60 << 20),
        cost_estimate=pl.CostEstimate(
            flops=12 * nt * rows * width * fw + 6 * rows * width * width,
            bytes_accessed=30 << 20,
            transcendentals=nt * rows * fw,
        ),
        name="middle",
    )(heads, resid, cot, wp, wi, wo, vec, fvec)


def halve(x, dim, axis, bit):
    n = lax.axis_size(axis)
    mine = (lax.axis_index(axis) // bit) % 2
    kept = lax.dynamic_index_in_dim(x, mine, dim, keepdims=False)
    sent = lax.dynamic_index_in_dim(x, 1 - mine, dim, keepdims=False)
    came = lax.ppermute(sent, axis, [(i, i ^ bit) for i in range(n)])
    return (kept.astype(F32) + came.astype(F32)).astype(x.dtype)


def bits_of(n):
    return [1 << i for i in range(n.bit_length() - 1)]


def scatter_sum(x, order):
    names = [("batch", b) for b in reversed(bits_of(lax.axis_size("batch")))]
    names += [("tensor", b) for b in reversed(bits_of(lax.axis_size("tensor")))]
    x = x.reshape((2,) * len(names) + x.shape[2:])
    for step in order:
        dim = names.index(step)
        x = halve(x, dim, *step)
        names.pop(dim)
    return x


def body(
    layer_input,
    doc_lengths,
    first_gain,
    first_shift,
    w_query,
    w_key,
    w_value,
    query_bias,
    value_bias,
    inner_gain,
    inner_shift,
    w_proj,
    proj_bias,
    second_gain,
    second_shift,
    w_in,
    in_bias,
    hidden_gain,
    hidden_shift,
    w_out,
    out_bias,
    cotangent,
):
    nt = lax.axis_size("tensor")
    nb = lax.axis_size("batch")
    rank = lax.axis_index("tensor")
    rows, width = layer_input.shape
    hw = w_query.shape[1]
    fw = w_in.shape[1]
    lengths = doc_lengths[0]

    resid = layer_input.astype(F32)
    mean, first_inv = ln_stats(resid, width)
    first_hat = (resid - mean) * first_inv
    first_low = (first_hat * first_gain.astype(F32) + first_shift.astype(F32)).astype(BF16)
    gathered = lax.all_gather(first_low, "tensor", axis=0, tiled=True)
    group_rows = gathered.shape[0]

    small = jnp.concatenate([in_bias, hidden_gain, hidden_shift, inner_gain, inner_shift])
    gathered, small, w_proj, w_in_, w_out_ = lax.optimization_barrier(
        (gathered, small, w_proj, w_in, w_out)
    )
    small_all = lax.all_gather(small, "tensor", axis=0)
    wp_all = lax.all_gather(w_proj, "tensor", axis=0, tiled=True)
    wi_all = lax.all_gather(w_in_, "tensor", axis=0)
    wo_all = lax.all_gather(w_out_, "tensor", axis=0)
    fvec = small_all[:, : 3 * fw].reshape(nt, 3, fw)
    inner_all = small_all[:, 3 * fw :].reshape(nt, 2, hw).transpose(1, 0, 2).reshape(2, width)
    vec = jnp.concatenate(
        [inner_all, jnp.stack([proj_bias, second_gain, second_shift, out_bias])], 0
    )

    wqkv = jnp.concatenate([w_query, w_key, w_value], 1)
    bqkv = jnp.concatenate([query_bias, jnp.zeros_like(query_bias), value_bias]).astype(F32)
    qkv = (dot_nn(gathered, wqkv) + bqkv).astype(BF16)
    heads, lse = attn_fwd(lengths, qkv, 512, 512)
    heads_all = lax.all_to_all(heads.reshape(nt, rows, hw), "tensor", 0, 0)
    layer_output, mixed_grad, heads_grad, g_in, g_out, g_proj, vsum, fsum = middle(
        heads_all, layer_input, cotangent, wp_all, wi_all, wo_all, vec, fvec, 256
    )
    grad_all = lax.all_to_all(heads_grad, "tensor", 0, 0).reshape(group_rows, hw)

    grads = jnp.concatenate([g_in, g_out, g_proj], 2)
    cols = grads.shape[2]
    grads = grads.reshape(nt, nb, width // nb, cols).transpose(1, 0, 2, 3)
    tbits = [("tensor", b) for b in bits_of(nt)]
    bbits = [("batch", b) for b in bits_of(nb)]
    total = scatter_sum(grads, tbits + bbits)

    dq, dk, dv = attn_bwd(lengths, qkv, heads, grad_all, lse, 512, 512)
    dqkv = jnp.concatenate([dq, dk, dv], 1)
    part = dot_nt(dqkv, wqkv).astype(BF16)
    first_grad = lax.psum_scatter(part, "tensor", scatter_dimension=0, tiled=True).astype(F32)
    g_qkv = lax.dot_general(
        gathered, dqkv, (((0,), (0,)), ((), ())), preferred_element_type=F32
    ).astype(BF16)
    g_qkv = g_qkv.reshape((2,) * len(bbits) + (width // nb, 3 * hw))
    names = list(reversed(bbits))
    for step in bbits:
        dim = names.index(step)
        g_qkv = halve(g_qkv, dim, *step)
        names.pop(dim)
    g_qkv = g_qkv.astype(F32)

    bias_sum = jnp.sum(dqkv.astype(F32), 0)
    grad_first_gain = jnp.sum(first_grad * first_hat, 0)
    grad_first_shift = jnp.sum(first_grad, 0)
    input_grad = mixed_grad + ln_back(
        first_grad * first_gain.astype(F32), first_hat, first_inv, width
    )

    def placed(piece):
        return lax.dynamic_update_slice(
            jnp.zeros((nt * piece.shape[0],), F32), piece, (rank * piece.shape[0],)
        )

    full = [
        grad_first_gain,
        grad_first_shift,
        placed(bias_sum[:hw]),
        placed(bias_sum[2 * hw :]),
        vsum[0],
        vsum[1],
        vsum[2],
        vsum[3],
        vsum[4],
        fsum[:, 0].reshape(-1),
        fsum[:, 1].reshape(-1),
        fsum[:, 2].reshape(-1),
        vsum[5],
    ]
    ndev = nb * nt
    packed = jnp.concatenate([v.reshape(ndev, -1) for v in full], 1)
    packed = packed.reshape(nb, nt, -1)
    packed = scatter_sum(packed, tbits + bbits)
    vectors = []
    at = 0
    for v in full:
        size = v.shape[0] // ndev
        vectors.append(packed[at : at + size])
        at += size

    total = total.astype(F32)
    return (
        layer_output,
        input_grad,
        vectors[0],
        vectors[1],
        g_qkv[:, :hw],
        g_qkv[:, hw : 2 * hw],
        g_qkv[:, 2 * hw :],
        vectors[2],
        vectors[3],
        vectors[4],
        vectors[5],
        total[:, 2 * fw :].T,
        vectors[6],
        vectors[7],
        vectors[8],
        total[:, :fw],
        vectors[9],
        vectors[10],
        vectors[11],
        total[:, fw : 2 * fw].T,
        vectors[12],
    )


def solution(mesh):
    both = ("batch", "tensor")
    in_specs = (
        P(both, None),
        P("batch", None),
        P(),
        P(),
        P(None, "tensor"),
        P(None, "tensor"),
        P(None, "tensor"),
        P("tensor"),
        P("tensor"),
        P("tensor"),
        P("tensor"),
        P("tensor", None),
        P(),
        P(),
        P(),
        P(None, "tensor"),
        P("tensor"),
        P("tensor"),
        P("tensor"),
        P("tensor", None),
        P(),
        P(both, None),
    )
    vector = P(both)
    out_specs = (
        P(both, None),
        P(both, None),
        vector,
        vector,
        P("batch", "tensor"),
        P("batch", "tensor"),
        P("batch", "tensor"),
        vector,
        vector,
        vector,
        vector,
        P("tensor", "batch"),
        vector,
        vector,
        vector,
        P("batch", "tensor"),
        vector,
        vector,
        vector,
        P("tensor", "batch"),
        vector,
    )
    return jax.shard_map(body, mesh=mesh, in_specs=in_specs, out_specs=out_specs, check_vma=False)
```

```python
import functools
import math

import jax
import jax.numpy as jnp
from jax import lax
from jax.experimental import pallas as pl
from jax.experimental.pallas import tpu as pltpu
from jax.sharding import PartitionSpec as P

HDIM = 64
EPS = 1e-05
SCALE = 0.125
LOG2E = 1.4426950408889634
NEG = -1e30
F32 = jnp.float32
BF16 = jnp.bfloat16


def dot_nn(a, b):
    return jnp.dot(a, b, preferred_element_type=F32)


def dot_nt(a, b):
    return lax.dot_general(a, b, (((1,), (1,)), ((), ())), preferred_element_type=F32)


def doc_ends(len_ref):
    ends = []
    total = jnp.int32(0)
    for i in range(len_ref.shape[0]):
        total = total + len_ref[i]
        ends.append(total)
    return ends


def doc_start(ends, pos):
    start = jnp.zeros_like(pos)
    for e in ends[:-1]:
        start = jnp.where(pos >= e, e, start)
    return start


def block_ranges(ends, q0, tq, tk):
    first = doc_start(ends, q0)
    last = doc_start(ends, q0 + tq - 1)
    lo = first // tk
    hi = (q0 + tq + tk - 1) // tk
    mid_lo = jnp.minimum((last + tk - 1) // tk, hi)
    mid_hi = jnp.maximum(q0 // tk, mid_lo)
    return lo, mid_lo, mid_hi, hi


def attn_fwd_kernel(tq, tk, nh, len_ref, qkv_ref, out_ref, lse_ref, k_s, v_s):
    step = pl.program_id(0)
    width = nh * HDIM
    total = k_s.shape[1]

    @pl.when(step == 0)
    def _():
        for h in range(nh):
            k_s[h] = qkv_ref[:, width + h * HDIM : width + (h + 1) * HDIM]
            vals = qkv_ref[:, 2 * width + h * HDIM : 2 * width + (h + 1) * HDIM]
            v_s[h, :HDIM, :] = vals.T
            v_s[h, HDIM:, :] = jnp.ones((16, total), BF16)

    q0 = pl.multiple_of(step * tq, tq)
    ends = doc_ends(len_ref)
    lo, mid_lo, mid_hi, hi = block_ranges(ends, q0, tq, tk)
    rows = qkv_ref[pl.ds(q0, tq), 0:width]
    queries = [rows[:, h * HDIM : (h + 1) * HDIM] for h in range(nh)]
    qpos = q0 + lax.broadcasted_iota(jnp.int32, (1, tq), 1)
    qstart = doc_start(ends, qpos)

    def one(masked, kb, carry):
        k0 = pl.multiple_of(kb * tk, tk)
        if masked:
            kpos = k0 + lax.broadcasted_iota(jnp.int32, (tk, tq), 0)
            allowed = (kpos >= qstart) & (kpos <= qpos)
        result = []
        for h in range(nh):
            peak, acc = carry[h]
            s = dot_nt(k_s[h, pl.ds(k0, tk), :], queries[h]) * (SCALE * LOG2E)
            if masked:
                s = jnp.where(allowed, s, NEG)
            new = jnp.maximum(peak, jnp.max(s, 0, keepdims=True))
            p = jnp.exp2(s - new).astype(BF16)
            acc = acc * jnp.exp2(peak - new) + dot_nn(v_s[h, :, pl.ds(k0, tk)], p)
            result.append((new, acc))
        return tuple(result)

    carry = tuple(
        (jnp.full((1, tq), NEG, F32), jnp.zeros((HDIM + 16, tq), F32)) for _ in range(nh)
    )
    carry = lax.fori_loop(lo, mid_lo, functools.partial(one, True), carry)
    carry = lax.fori_loop(mid_lo, mid_hi, functools.partial(one, False), carry)
    carry = lax.fori_loop(mid_hi, hi, functools.partial(one, True), carry)
    for h in range(nh):
        peak, acc = carry[h]
        total_row = acc[HDIM : HDIM + 1]
        out_ref[h * HDIM : (h + 1) * HDIM, :] = (acc[:HDIM] / total_row).astype(BF16)
        lse_ref[h : h + 1, :] = peak + jnp.log2(total_row)


def attn_fwd(lengths, qkv, tq, tk):
    rows, width3 = qkv.shape
    width = width3 // 3
    nh = width // HDIM
    return pl.pallas_call(
        functools.partial(attn_fwd_kernel, tq, tk, nh),
        out_shape=(
            jax.ShapeDtypeStruct((width, rows), BF16),
            jax.ShapeDtypeStruct((nh, rows), F32),
        ),
        grid_spec=pltpu.PrefetchScalarGridSpec(
            num_scalar_prefetch=1,
            grid=(rows // tq,),
            in_specs=[pl.BlockSpec((rows, width3), lambda i, l: (0, 0))],
            out_specs=(
                pl.BlockSpec((width, tq), lambda i, l: (0, i)),
                pl.BlockSpec((nh, tq), lambda i, l: (0, i)),
            ),
            scratch_shapes=[
                pltpu.VMEM((nh, rows, HDIM), BF16),
                pltpu.VMEM((nh, HDIM + 16, rows), BF16),
            ],
        ),
        compiler_params=pltpu.CompilerParams(vmem_limit_bytes=48 << 20),
        cost_estimate=pl.CostEstimate(
            flops=2 * 2 * nh * HDIM * rows * rows // 2,
            bytes_accessed=rows * width3 * 2 + rows * width * 2,
            transcendentals=nh * rows * rows // 2,
        ),
        name="attn_fwd",
    )(lengths, qkv)


def attn_bwd_kernel(
    tq, tk, nh, len_ref, qkv_ref, out_ref, grad_ref, lse_ref, dqkv_ref,
    k_s, kt_s, v_s, dk_s, dv_s,
):
    step = pl.program_id(0)
    width = nh * HDIM
    total = k_s.shape[1]

    @pl.when(step == 0)
    def _():
        for h in range(nh):
            keys = qkv_ref[:, width + h * HDIM : width + (h + 1) * HDIM]
            k_s[h] = keys
            kt_s[h] = keys.T
            v_s[h] = qkv_ref[:, 2 * width + h * HDIM : 2 * width + (h + 1) * HDIM]
        dk_s[...] = jnp.zeros_like(dk_s)
        dv_s[...] = jnp.zeros_like(dv_s)

    q0 = pl.multiple_of(step * tq, tq)
    ends = doc_ends(len_ref)
    lo, mid_lo, mid_hi, hi = block_ranges(ends, q0, tq, tk)
    rows = qkv_ref[pl.ds(q0, tq), 0:width]
    queries = [rows[:, h * HDIM : (h + 1) * HDIM] for h in range(nh)]
    grads_t = [grad_ref[h * HDIM : (h + 1) * HDIM, :] for h in range(nh)]
    grads = [g.T for g in grads_t]
    prod = grad_ref[...].astype(F32) * out_ref[...].astype(F32)
    deltas = [
        jnp.sum(prod[h * HDIM : (h + 1) * HDIM], 0, keepdims=True) for h in range(nh)
    ]
    lses = [lse_ref[h : h + 1, :] for h in range(nh)]
    qpos = q0 + lax.broadcasted_iota(jnp.int32, (1, tq), 1)
    qstart = doc_start(ends, qpos)

    def one(masked, kb, carry):
        k0 = pl.multiple_of(kb * tk, tk)
        if masked:
            kpos = k0 + lax.broadcasted_iota(jnp.int32, (tk, tq), 0)
            allowed = (kpos >= qstart) & (kpos <= qpos)
        result = []
        for h in range(nh):
            s = dot_nt(k_s[h, pl.ds(k0, tk), :], queries[h]) * (SCALE * LOG2E)
            if masked:
                s = jnp.where(allowed, s, NEG)
            p = jnp.exp2(s - lses[h])
            dp = dot_nn(v_s[h, pl.ds(k0, tk), :], grads_t[h])
            ds = (p * (dp - deltas[h])).astype(BF16)
            dv_s[h, pl.ds(k0, tk), :] += dot_nn(p.astype(BF16), grads[h])
            dk_s[h, pl.ds(k0, tk), :] += dot_nn(ds, queries[h])
            result.append(carry[h] + dot_nn(kt_s[h, :, pl.ds(k0, tk)], ds))
        return tuple(result)

    carry = tuple(jnp.zeros((HDIM, tq), F32) for _ in range(nh))
    carry = lax.fori_loop(lo, mid_lo, functools.partial(one, True), carry)
    carry = lax.fori_loop(mid_lo, mid_hi, functools.partial(one, False), carry)
    carry = lax.fori_loop(mid_hi, hi, functools.partial(one, True), carry)
    dq = (jnp.concatenate(carry, 0) * SCALE).astype(BF16)
    dqkv_ref[pl.ds(q0, tq), 0:width] = dq.T

    @pl.when(step == pl.num_programs(0) - 1)
    def _():
        for h in range(nh):
            at = width + h * HDIM
            dqkv_ref[:, at : at + HDIM] = (dk_s[h] * SCALE).astype(BF16)
            dqkv_ref[:, width + at : width + at + HDIM] = dv_s[h].astype(BF16)


def attn_bwd(lengths, qkv, out, grad, lse, tq, tk):
    rows, width3 = qkv.shape
    width = width3 // 3
    nh = width // HDIM
    return pl.pallas_call(
        functools.partial(attn_bwd_kernel, tq, tk, nh),
        out_shape=jax.ShapeDtypeStruct((rows, width3), BF16),
        grid_spec=pltpu.PrefetchScalarGridSpec(
            num_scalar_prefetch=1,
            grid=(rows // tq,),
            in_specs=[
                pl.BlockSpec((rows, width3), lambda i, l: (0, 0)),
                pl.BlockSpec((width, tq), lambda i, l: (0, i)),
                pl.BlockSpec((width, tq), lambda i, l: (0, i)),
                pl.BlockSpec((nh, tq), lambda i, l: (0, i)),
            ],
            out_specs=pl.BlockSpec((rows, width3), lambda i, l: (0, 0)),
            scratch_shapes=[
                pltpu.VMEM((nh, rows, HDIM), BF16),
                pltpu.VMEM((nh, HDIM, rows), BF16),
                pltpu.VMEM((nh, rows, HDIM), BF16),
                pltpu.VMEM((nh, rows, HDIM), F32),
                pltpu.VMEM((nh, rows, HDIM), F32),
            ],
        ),
        compiler_params=pltpu.CompilerParams(vmem_limit_bytes=56 << 20),
        cost_estimate=pl.CostEstimate(
            flops=5 * 2 * nh * HDIM * rows * rows // 2,
            bytes_accessed=rows * width3 * 4,
            transcendentals=nh * rows * rows // 2,
        ),
        name="attn_bwd",
    )(lengths, qkv, out, grad, lse)


MESH = pl.DeviceIdType.MESH
ROWS = 256


def flip1(i):
    return i + 1 - 2 * (i % 2)


def flip2(i):
    return i + 2 - 4 * ((i // 2) % 2)


def flips(t):
    return [t, flip1(t), flip2(t), flip1(flip2(t))]


def flip_bit(i, bit):
    return i + bit - 2 * bit * ((i // bit) % 2)


def greet(partners):
    barrier = pltpu.get_barrier_semaphore()
    for p in partners:
        pl.semaphore_signal(barrier, inc=1, device_id=p, device_id_type=MESH)
    pl.semaphore_wait(barrier, len(partners))


def copier(send, recv):
    def copy(src, dst, i, dev):
        return pltpu.make_async_remote_copy(
            src_ref=src,
            dst_ref=dst,
            send_sem=send.at[i],
            recv_sem=recv.at[i],
            device_id=dev,
            device_id_type=MESH,
        )

    return copy


def bits_of(n):
    return [1 << i for i in range(n.bit_length() - 1)]


def ln_stats(v, n):
    mean = jnp.sum(v, -1, keepdims=True) * (1.0 / n)
    var = jnp.sum(v * v, -1, keepdims=True) * (1.0 / n) - mean * mean
    return mean, lax.rsqrt(var + EPS)


def ln_back(dh, hat, inv, n):
    m0 = jnp.sum(dh, -1, keepdims=True) * (1.0 / n)
    m1 = jnp.sum(dh * hat, -1, keepdims=True) * (1.0 / n)
    return inv * (dh - m0 - hat * m1)


def col_sum(v):
    return jnp.sum(v, 0, keepdims=True)


def front_kernel(
    x_ref, vec_ref, wqkv_ref, bqkv_ref, wi_ref, wo_ref, wp_ref, sm_ref,
    qkv_ref, nt_ref, wi_all, wo_all, wp_all, sm_all,
    nrm, send, recv,
):
    b = lax.axis_index("batch")
    t = lax.axis_index("tensor")
    ranks = flips(t)
    core, across = (b, ranks[1]), (b, ranks[2])
    side, near = (flip1(b), t), (flip2(b), t)
    rows = x_ref.shape[0]
    chunks = rows // ROWS
    copy = copier(send, recv)
    greet([core, across, side, near])

    weights = [(wi_ref, wi_all), (wo_ref, wo_all), (wp_ref, wp_all)]
    order = [2, 0, 1]
    quarter = b % 4
    parts = [quarter, flip1(quarter), flip2(quarter), flip1(flip2(quarter))]

    def part(a, ref, q):
        depth = weights[a][0].shape[0] // 4
        return ref.at[pl.ds(pl.multiple_of(parts[q] * depth, depth), depth)]

    sends = []

    def go(c):
        c.start()
        sends.append(c)
        return c

    first = {}
    for a in order:
        src, dst = weights[a]
        first[a] = go(copy(part(a, src, 0), part(a, dst.at[1], 0), a, across))
    small_x = go(copy(sm_ref, sm_all.at[1], 3, across))
    whole = []
    for a in order:
        src, dst = weights[a]
        whole.append(go(copy(src, dst.at[0], 4 + a, core)))
    whole.append(go(copy(sm_ref, sm_all.at[0], 7, core)))

    gain = vec_ref[0:1, :].astype(F32)
    shift = vec_ref[1:2, :].astype(F32)

    def project(j, k):
        at = pl.ds(pl.multiple_of(ranks[j] * rows + k * ROWS, ROWS), ROWS)
        low = nrm[j, k * ROWS : (k + 1) * ROWS, :]
        qkv_ref[at, :] = (dot_nn(low, wqkv_ref[...]) + bqkv_ref[...]).astype(BF16)
        nt_ref[:, at] = low.T

    def chunk(j, k):
        return nrm.at[j, pl.ds(k * ROWS, ROWS)]

    near_by = []
    for k in range(chunks):
        v = x_ref[k * ROWS : (k + 1) * ROWS, :].astype(F32)
        mean, inv = ln_stats(v, v.shape[1])
        nrm[0, k * ROWS : (k + 1) * ROWS, :] = ((v - mean) * inv * gain + shift).astype(BF16)
        near_by.append(go(copy(chunk(0, k), chunk(1, k), 8 + k, core)))
    for a in order:
        first[a].wait_send()
    far = []
    for k in range(chunks):
        far.append(go(copy(chunk(0, k), chunk(2, k), 8 + chunks + k, across)))
    base = 8 + 3 * chunks

    def pass_on(a, q):
        ref = part(a, weights[a][1].at[1], q)
        if q == 0:
            go(copy(ref, ref, base + a, side))
        if q < 2:
            go(copy(ref, ref, base + 3 + 2 * a + q, near))
        go(copy(ref, part(a, weights[a][1].at[2], q), base + 9 + 4 * a + q, core))

    def from_side(a):
        ref = part(a, weights[a][1].at[1], 1)
        copy(ref, ref, base + a, side).wait_recv()
        pass_on(a, 1)

    def from_near(a, q):
        ref = part(a, weights[a][1].at[1], q + 2)
        copy(ref, ref, base + 3 + 2 * a + q, near).wait_recv()
        pass_on(a, q + 2)

    def far_chunk(k):
        far[k].wait_recv()
        go(copy(chunk(2, k), chunk(3, k), 8 + 2 * chunks + k, core))
        project(2, k)

    for k in range(chunks):
        project(0, k)
    for a in order:
        first[a].wait_recv()
        pass_on(a, 0)
    small_x.wait_recv()
    small_d = go(copy(sm_all.at[1], sm_all.at[2], base + 21, core))
    for k in range(chunks):
        near_by[k].wait_recv()
        project(1, k)
    for a in order:
        from_side(a)
    for k in range(chunks):
        far_chunk(k)
        if k == 0:
            for a in order:
                from_near(a, 0)
    for a in order:
        from_near(a, 1)
    for k in range(chunks):
        copy(chunk(2, k), chunk(3, k), 8 + 2 * chunks + k, core).wait_recv()
        project(3, k)
    small_d.wait_recv()
    for c in whole:
        c.wait_recv()
    for a in order:
        for q in range(4):
            ref = part(a, weights[a][1].at[2], q)
            copy(ref, ref, base + 9 + 4 * a + q, core).wait_recv()
    done = set(id(first[a]) for a in order)
    for c in sends:
        if id(c) not in done:
            c.wait_send()


def front(x, vec, wqkv, bqkv, wi, wo, wp, sm, nt):
    rows, width = x.shape
    group = rows * nt
    sems = 8 + 3 * (rows // ROWS) + 22
    vmem = pl.BlockSpec(memory_space=pltpu.VMEM)
    hbm = pl.BlockSpec(memory_space=pl.ANY)
    shape = jax.ShapeDtypeStruct
    return pl.pallas_call(
        front_kernel,
        out_shape=(
            shape((group, wqkv.shape[1]), BF16),
            shape((width, group), BF16),
            shape((nt - 1,) + wi.shape, BF16),
            shape((nt - 1,) + wo.shape, BF16),
            shape((nt - 1,) + wp.shape, BF16),
            shape((nt - 1,) + sm.shape, BF16),
        ),
        in_specs=[vmem] * 4 + [hbm] * 4,
        out_specs=(vmem, vmem) + (hbm,) * 4,
        scratch_shapes=[
            pltpu.VMEM((nt, rows, width), BF16),
            pltpu.SemaphoreType.DMA((sems,)),
            pltpu.SemaphoreType.DMA((sems,)),
        ],
        compiler_params=pltpu.CompilerParams(
            collective_id=0, has_side_effects=True, vmem_limit_bytes=48 << 20
        ),
        cost_estimate=pl.CostEstimate(
            flops=2 * group * width * wqkv.shape[1], bytes_accessed=20 << 20, transcendentals=0
        ),
        name="front",
    )(x, vec, wqkv, bqkv, wi, wo, wp, sm)


def mid_kernel(
    tm, nt,
    heads_ref, resid_ref, cot_ref, wi_own, wo_own, wp_own, wi_all, wo_all, wp_all,
    sm_own, sm_all, vec_ref,
    lout_ref, mg_ref, hg_all, ra_ref, rb_ref, vs_ref, fs_ref,
    wi_s, wo_s, wp_s, hr_s, hg_s, act_s, dact_s, dh_s, hid_s, pre_s, inner_s,
    sec_t, cot_t, att_t, gsa, gsb, gra, grb, send, recv, local,
):
    b = lax.axis_index("batch")
    t = lax.axis_index("tensor")
    ranks = flips(t)
    devs = [(b, r) for r in ranks]
    step = pl.program_id(0)
    tiles = pl.num_programs(0) - nt
    n_tiles = hr_s.shape[2] // tm
    rows = n_tiles * tm
    width = resid_ref.shape[1]
    fw = wi_s.shape[2]
    ff = nt * fw
    hw = width // nt
    copy = copier(send, recv)

    def sm_row(j, i):
        ref = sm_own if j == 0 else sm_all.at[j - 1]
        return ref[i : i + 1, :].astype(F32)

    def lanes(rank, r):
        return pl.ds(pl.multiple_of(rank * rows + r * tm, tm), tm)

    def heads_in(j, r):
        return copy(
            heads_ref.at[:, lanes(ranks[j], r)],
            hr_s.at[j, :, pl.ds(pl.multiple_of(r * tm, tm), tm)],
            j * n_tiles + r,
            devs[j],
        )

    def own_heads():
        return pltpu.make_async_copy(
            heads_ref.at[:, pl.ds(pl.multiple_of(t * rows, tm), rows)], hr_s.at[0], local.at[0]
        )

    def grads_out(j, r):
        return copy(
            hg_s.at[j, :, pl.ds(pl.multiple_of(r * tm, tm), tm)],
            hg_all.at[:, lanes(t, r)],
            (nt + j) * n_tiles + r,
            devs[j],
        )

    def own_grads():
        return pltpu.make_async_copy(
            hg_s.at[0], hg_all.at[:, pl.ds(pl.multiple_of(t * rows, tm), rows)], local.at[1]
        )

    base = 2 * nt * n_tiles

    def sum_a(s):
        return copy(gsa.at[s], gra.at[s], base + s, devs[1])

    def sum_b(s):
        return copy(gsb.at[s], grb.at[s], base + 2 + s, devs[1])

    def out_a(s):
        return pltpu.make_async_copy(gra.at[s], ra_ref.at[s], local.at[2 + s])

    def out_b(s):
        return pltpu.make_async_copy(grb.at[s], rb_ref.at[s], local.at[4 + s])

    def loads(own, rest, dst, i):
        return [
            pltpu.make_async_copy(own, dst.at[0], local.at[6 + 2 * i]),
            pltpu.make_async_copy(rest, dst.at[pl.ds(1, nt - 1)], local.at[7 + 2 * i]),
        ]

    load_p = loads(wp_own, wp_all, wp_s, 0)
    load_i = loads(wi_own, wi_all, wi_s, 1)
    load_o = loads(wo_own, wo_all, wo_s, 2)

    @pl.when(step == 0)
    def _():
        for c in load_p + load_i + load_o:
            c.start()
        own_heads().start()
        greet(devs[1:])
        for r in range(n_tiles):
            for j in (2, 3, 1):
                heads_in(j, r).start()
        vs_ref[...] = jnp.zeros_like(vs_ref)
        fs_ref[...] = jnp.zeros_like(fs_ref)
        for c in load_p:
            c.wait()
        own_heads().wait()

    @pl.when(step < tiles)
    def _():
        r0 = pl.multiple_of(step * tm, tm)
        here = pl.ds(r0, tm)
        for j in range(1, nt):
            heads_in(j, step).wait_recv()
        proj_bias, second_gain, second_shift, out_bias = [
            vec_ref[i : i + 1, :].astype(F32) for i in range(4)
        ]
        tails = [sm_row(j, 3) for j in range(nt)]
        inner_gain = jnp.concatenate([v[:, :hw] for v in tails], 1)
        inner_shift = jnp.concatenate([v[:, hw : 2 * hw] for v in tails], 1)
        heads = jnp.concatenate([hr_s[j, :, here] for j in range(nt)], 0).T.astype(F32)
        mean, inner_inv = ln_stats(heads, width)
        inner_hat = (heads - mean) * inner_inv
        inner_low = (inner_hat * inner_gain + inner_shift).astype(BF16)
        for j in range(nt):
            inner_s[j, here, :] = inner_low[:, j * hw : (j + 1) * hw]
        wp = jnp.concatenate([wp_s[j] for j in range(nt)], 0)
        mixed = resid_ref[...].astype(F32) + (dot_nn(inner_low, wp) + proj_bias)
        mean, second_inv = ln_stats(mixed, width)
        second_hat = (mixed - mean) * second_inv
        second_low = (second_hat * second_gain + second_shift).astype(BF16)
        sec_t[:, here] = second_low.T
        cot_low = cot_ref[...]
        cot_t[:, here] = cot_low.T
        cot = cot_low.astype(F32)

        @pl.when(step == 0)
        def _():
            for c in load_i:
                c.wait()

        c0 = math.sqrt(2.0 / math.pi)
        c1 = 0.044715
        s0 = jnp.zeros((tm, 1), F32)
        s1 = jnp.zeros((tm, 1), F32)
        for j in range(nt):
            v = dot_nn(second_low, wi_s[j]) + sm_row(j, 0)
            v2 = v * v
            th = jnp.tanh(v * (c0 + (c0 * c1) * v2))
            half = 0.5 + 0.5 * th
            act = v * half
            dact = half + (0.5 * v) * (1.0 - th * th) * (c0 + (3.0 * c0 * c1) * v2)
            act_s[j] = act
            dact_s[j] = dact
            s0 += jnp.sum(act, -1, keepdims=True)
            s1 += jnp.sum(act * act, -1, keepdims=True)
        mean = s0 * (1.0 / ff)
        inv = lax.rsqrt(s1 * (1.0 / ff) - mean * mean + EPS)
        result = mixed + out_bias
        m0 = jnp.zeros((tm, 1), F32)
        m1 = jnp.zeros((tm, 1), F32)

        @pl.when(step == 0)
        def _():
            for c in load_o:
                c.wait()

        for j in range(nt):
            gain = sm_row(j, 1)
            hat = (act_s[j] - mean) * inv
            act_s[j] = hat
            hid = (hat * gain + sm_row(j, 2)).astype(BF16)
            hid_s[j, here, :] = hid
            result += dot_nn(hid, wo_s[j])
            gh = dot_nt(cot_low, wo_s[j])
            gn = gh * hat
            fs_ref[j, 1:2, :] += col_sum(gn)
            fs_ref[j, 2:3, :] += col_sum(gh)
            dh = gh * gain
            dh_s[j] = dh
            m0 += jnp.sum(dh, -1, keepdims=True)
            m1 += jnp.sum(gn * gain, -1, keepdims=True)
        lout_ref[...] = result.astype(BF16)
        m0 = m0 * (1.0 / ff)
        m1 = m1 * (1.0 / ff)
        second_grad = jnp.zeros((tm, width), F32)
        for j in range(nt):
            pre = (inv * (dh_s[j] - m0 - act_s[j] * m1) * dact_s[j]).astype(BF16)
            pre_s[j, here, :] = pre
            fs_ref[j, 0:1, :] += col_sum(pre.astype(F32))
            second_grad += dot_nt(pre, wi_s[j])
        vs_ref[3:4, :] += col_sum(second_grad * second_hat)
        vs_ref[4:5, :] += col_sum(second_grad)
        vs_ref[5:6, :] += col_sum(cot)
        mixed_grad = cot + ln_back(second_grad * second_gain, second_hat, second_inv, width)
        mg_ref[...] = mixed_grad
        vs_ref[2:3, :] += col_sum(mixed_grad)
        att = mixed_grad.astype(BF16)
        att_t[:, here] = att.T
        grad_inner = dot_nt(att, wp)
        vs_ref[0:1, :] += col_sum(grad_inner * inner_hat)
        vs_ref[1:2, :] += col_sum(grad_inner)
        hg = ln_back(grad_inner * inner_gain, inner_hat, inner_inv, width).astype(BF16).T
        for j in range(nt):
            hg_s[j, :, here] = hg[j * hw : (j + 1) * hw, :]
        for j in (2, 3, 1):
            grads_out(j, step).start()

    @pl.when(step == tiles)
    def _():
        own_grads().start()

    @pl.when((step >= tiles) & (step < tiles + 2))
    def _():
        s = step - tiles
        j = 2 * s + 1
        gsa[s, :, :fw] = dot_nn(sec_t[...], pre_s[j]).astype(BF16)
        gsa[s, :, fw:] = dot_nn(att_t[...], inner_s[j]).astype(BF16)
        sum_a(s).start()
        gsb[s] = dot_nn(cot_t[...], hid_s[j]).astype(BF16)
        sum_b(s).start()

    @pl.when(step >= tiles + 2)
    def _():
        s = step - tiles - 2
        j = 2 * s
        ga = dot_nn(sec_t[...], pre_s[j])
        gp = dot_nn(att_t[...], inner_s[j])
        sum_a(s).wait_recv()
        gra[s, :, :fw] = (ga + gra[s, :, :fw].astype(F32)).astype(BF16)
        gra[s, :, fw:] = (gp + gra[s, :, fw:].astype(F32)).astype(BF16)
        out_a(s).start()
        gb = dot_nn(cot_t[...], hid_s[j])
        sum_b(s).wait_recv()
        grb[s] = (gb + grb[s].astype(F32)).astype(BF16)
        out_b(s).start()

    @pl.when(step == pl.num_programs(0) - 1)
    def _():
        own_grads().wait()
        for r in range(n_tiles):
            for j in range(1, nt):
                heads_in(j, r).wait_send()
                grads_out(j, r).wait_send()
                grads_out(j, r).wait_recv()
        for s in range(2):
            sum_a(s).wait_send()
            sum_b(s).wait_send()
            out_a(s).wait()
            out_b(s).wait()


def middle(heads, resid, cot, own, gathered, vec, tm, nt):
    wi, wo, wp, sm = own
    hw, group = heads.shape
    rows, width = resid.shape
    fw = wi.shape[1]
    tiles = rows // tm
    last = tiles - 1
    tile = lambda i: jnp.minimum(i, last)
    hbm = pl.BlockSpec(memory_space=pl.ANY)
    vmem = pl.BlockSpec(memory_space=pltpu.VMEM)
    shape = jax.ShapeDtypeStruct
    block = pl.BlockSpec((tm, width), lambda i: (tile(i), 0))
    sems = 2 * nt * tiles + 4
    return pl.pallas_call(
        functools.partial(mid_kernel, tm, nt),
        out_shape=(
            shape((rows, width), BF16),
            shape((rows, width), F32),
            shape((hw, group), BF16),
            shape((2, width, fw + hw), BF16),
            shape((2, width, fw), BF16),
            shape((8, width), F32),
            shape((nt, 8, fw), F32),
        ),
        grid=(tiles + nt,),
        in_specs=[hbm, block, block] + [hbm] * 6 + [vmem] * 3,
        out_specs=(block, block, hbm, hbm, hbm, vmem, vmem),
        scratch_shapes=[
            pltpu.VMEM((nt,) + wi.shape, BF16),
            pltpu.VMEM((nt,) + wo.shape, BF16),
            pltpu.VMEM((nt,) + wp.shape, BF16),
            pltpu.VMEM((nt, hw, rows), BF16),
            pltpu.VMEM((nt, hw, rows), BF16),
            pltpu.VMEM((nt, tm, fw), F32),
            pltpu.VMEM((nt, tm, fw), F32),
            pltpu.VMEM((nt, tm, fw), F32),
            pltpu.VMEM((nt, rows, fw), BF16),
            pltpu.VMEM((nt, rows, fw), BF16),
            pltpu.VMEM((nt, rows, hw), BF16),
            pltpu.VMEM((width, rows), BF16),
            pltpu.VMEM((width, rows), BF16),
            pltpu.VMEM((width, rows), BF16),
            pltpu.VMEM((2, width, fw + hw), BF16),
            pltpu.VMEM((2, width, fw), BF16),
            pltpu.VMEM((2, width, fw + hw), BF16),
            pltpu.VMEM((2, width, fw), BF16),
            pltpu.SemaphoreType.DMA((sems,)),
            pltpu.SemaphoreType.DMA((sems,)),
            pltpu.SemaphoreType.DMA((12,)),
        ],
        compiler_params=pltpu.CompilerParams(
            collective_id=1, has_side_effects=True, vmem_limit_bytes=62 << 20
        ),
        cost_estimate=pl.CostEstimate(
            flops=12 * nt * rows * width * fw + 6 * rows * width * width,
            bytes_accessed=30 << 20,
            transcendentals=nt * rows * fw,
        ),
        name="middle",
    )(heads, resid, cot, wi, wo, wp, *gathered[:3], sm, gathered[3], vec)


def tail_kernel(
    nt, nb,
    dqkv_ref, nt_ref, wqkv_ref, x_ref, mg_ref, vec_ref,
    ig_ref, gq_ref, fv_ref, bias_ref,
    core_s, core_r, far_s, far_r, acc_s, cur, came, send, recv,
):
    b = lax.axis_index("batch")
    t = lax.axis_index("tensor")
    ranks = flips(t)
    core, across = (b, ranks[1]), (b, ranks[2])
    bits = bits_of(nb)
    others = [(flip_bit(b, bit), t) for bit in bits]
    rows, width = x_ref.shape
    chunks = rows // ROWS
    copy = copier(send, recv)
    greet([core, across] + others)

    def part(j, k):
        at = pl.ds(pl.multiple_of(ranks[j] * rows + k * ROWS, ROWS), ROWS)
        return dot_nt(dqkv_ref[at, :], wqkv_ref[...])

    def to_core(i, k):
        at = pl.ds(k * ROWS, ROWS)
        return copy(core_s.at[i, at], core_r.at[i, at], i * chunks + k, core)

    def to_far(k):
        at = pl.ds(k * ROWS, ROWS)
        return copy(far_s.at[at], far_r.at[at], 2 * chunks + k, across)

    def rows_of(k):
        return slice(k * ROWS, (k + 1) * ROWS)

    for k in range(chunks):
        core_s[0, rows_of(k), :] = part(3, k).astype(BF16)
        to_core(0, k).start()
    for k in range(chunks):
        mine = part(2, k)
        to_core(0, k).wait_recv()
        far_s[rows_of(k), :] = (mine + core_r[0, rows_of(k), :].astype(F32)).astype(BF16)
        to_far(k).start()

    depth = width // nb
    half = [1 - (b // bit) % 2 for bit in bits]

    def swap(i):
        return copy(
            cur[i].at[:, pl.ds(half[i], 1)], came[i], 3 * chunks + i, others[i]
        )

    grad = dot_nn(nt_ref[...], dqkv_ref[...]).astype(BF16)
    for i in range(nb):
        cur[0][i // 2, i % 2] = grad[i * depth : (i + 1) * depth, :]
    swap(0).start()
    for k in range(chunks):
        core_s[1, rows_of(k), :] = part(1, k).astype(BF16)
        to_core(1, k).start()
    bias_ref[...] = jnp.zeros_like(bias_ref)
    for k in range(chunks * nt):
        bias_ref[0:1, :] += col_sum(dqkv_ref[k * ROWS : (k + 1) * ROWS, :].astype(F32))
    for k in range(chunks):
        mine = part(0, k)
        to_core(1, k).wait_recv()
        acc_s[rows_of(k), :] = mine + core_r[1, rows_of(k), :].astype(F32)

    gain = vec_ref[0:1, :].astype(F32)
    fv_ref[...] = jnp.zeros_like(fv_ref)

    def finish(k):
        to_far(k).wait_recv()
        grad = acc_s[rows_of(k), :] + far_r[rows_of(k), :].astype(F32)
        v = x_ref[rows_of(k), :].astype(F32)
        mean, inv = ln_stats(v, width)
        hat = (v - mean) * inv
        fv_ref[0:1, :] += col_sum(grad * hat)
        fv_ref[1:2, :] += col_sum(grad)
        ig_ref[rows_of(k), :] = mg_ref[rows_of(k), :] + ln_back(grad * gain, hat, inv, width)

    def add(i):
        swap(i).wait_recv()
        n = cur[i].shape[0]
        kept = cur[i][:, pl.ds(1 - half[i], 1)].astype(F32) + came[i][...].astype(F32)
        if i == len(bits) - 1:
            gq_ref[...] = kept[0, 0]
            return
        kept = kept.astype(BF16)
        for m in range(n):
            cur[i + 1][m // 2, m % 2] = kept[m, 0]
        swap(i + 1).start()

    left = list(range(chunks))
    for i in range(len(bits)):
        add(i)
        if left:
            finish(left.pop(0))
    for k in left:
        finish(k)
    for k in range(chunks):
        to_core(0, k).wait_send()
        to_core(1, k).wait_send()
        to_far(k).wait_send()
    for i in range(len(bits)):
        swap(i).wait_send()


def tail_entry(nt, nb, *refs):
    n = nb.bit_length() - 1
    fixed, cur, came = refs[:15], refs[15 : 15 + n], refs[15 + n : 15 + 2 * n]
    tail_kernel(nt, nb, *fixed, list(cur), list(came), *refs[15 + 2 * n :])


def tail(dqkv, normed_t, wqkv, x, mixed_grad, vec, nt, nb):
    rows, width = x.shape
    cols = wqkv.shape[1]
    depth = width // nb
    bits = bits_of(nb)
    shape = jax.ShapeDtypeStruct
    vmem = pl.BlockSpec(memory_space=pltpu.VMEM)
    sems = 3 * (rows // ROWS) + len(bits)
    return pl.pallas_call(
        functools.partial(tail_entry, nt, nb),
        out_shape=(
            shape((rows, width), F32),
            shape((depth, cols), F32),
            shape((8, width), F32),
            shape((8, cols), F32),
        ),
        in_specs=[vmem] * 6,
        out_specs=(vmem,) * 4,
        scratch_shapes=[
            pltpu.VMEM((2, rows, width), BF16),
            pltpu.VMEM((2, rows, width), BF16),
            pltpu.VMEM((rows, width), BF16),
            pltpu.VMEM((rows, width), BF16),
            pltpu.VMEM((rows, width), F32),
        ]
        + [pltpu.VMEM((nb // bit // 2, 2, depth, cols), BF16) for bit in bits]
        + [pltpu.VMEM((nb // bit // 2, 1, depth, cols), BF16) for bit in bits]
        + [pltpu.SemaphoreType.DMA((sems,)), pltpu.SemaphoreType.DMA((sems,))],
        compiler_params=pltpu.CompilerParams(
            collective_id=2, has_side_effects=True, vmem_limit_bytes=56 << 20
        ),
        cost_estimate=pl.CostEstimate(
            flops=4 * rows * nt * width * cols, bytes_accessed=20 << 20, transcendentals=0
        ),
        name="tail",
    )(dqkv, normed_t, wqkv, x, mixed_grad, vec)


def vector_kernel(nt, nb, packed_ref, out_ref, first_s, sum_s, second_s, send, recv):
    b = lax.axis_index("batch")
    t = lax.axis_index("tensor")
    ranks = flips(t)
    copy = copier(send, recv)
    group = [(b, r) for r in ranks]
    others = [((b + i) % nb, t) for i in range(nb)]
    greet(group[1:] + others[1:])

    def one(j):
        return copy(packed_ref.at[:, pl.ds(ranks[j], 1)], first_s.at[j], j, group[j])

    def two(i):
        return copy(sum_s.at[others[i][0]], second_s.at[i], nt + i, others[i])

    for j in range(1, nt):
        one(j).start()
    total = packed_ref[:, pl.ds(t, 1)]
    for j in range(1, nt):
        one(j).wait_recv()
        total += first_s[j]
    sum_s[...] = total[:, 0]
    for i in range(1, nb):
        two(i).start()
    total = sum_s[b]
    for i in range(1, nb):
        two(i).wait_recv()
        total += second_s[i]
    out_ref[...] = total
    for j in range(1, nt):
        one(j).wait_send()
    for i in range(1, nb):
        two(i).wait_send()


def vector_sums(packed):
    nb, nt, high, wide = packed.shape
    vmem = pl.BlockSpec(memory_space=pltpu.VMEM)
    return pl.pallas_call(
        functools.partial(vector_kernel, nt, nb),
        out_shape=jax.ShapeDtypeStruct((high, wide), F32),
        in_specs=[vmem],
        out_specs=vmem,
        scratch_shapes=[
            pltpu.VMEM((nt, nb, 1, high, wide), F32),
            pltpu.VMEM((nb, high, wide), F32),
            pltpu.VMEM((nb, high, wide), F32),
            pltpu.SemaphoreType.DMA((nt + nb,)),
            pltpu.SemaphoreType.DMA((nt + nb,)),
        ],
        compiler_params=pltpu.CompilerParams(collective_id=3, has_side_effects=True),
        name="vector_sums",
    )(packed)


def halve(x, dim, axis, bit):
    mine = (lax.axis_index(axis) // bit) % 2
    kept = lax.dynamic_index_in_dim(x, mine, dim, keepdims=False)
    sent = lax.dynamic_index_in_dim(x, 1 - mine, dim, keepdims=False)
    return (kept.astype(F32) + swapped(sent, axis, bit).astype(F32)).astype(x.dtype)


def swapped(x, axis, bit):
    return lax.ppermute(x, axis, [(i, i ^ bit) for i in range(lax.axis_size(axis))])


def body(
    layer_input,
    doc_lengths,
    first_gain,
    first_shift,
    w_query,
    w_key,
    w_value,
    query_bias,
    value_bias,
    inner_gain,
    inner_shift,
    w_proj,
    proj_bias,
    second_gain,
    second_shift,
    w_in,
    in_bias,
    hidden_gain,
    hidden_shift,
    w_out,
    out_bias,
    cotangent,
):
    nt = lax.axis_size("tensor")
    nb = lax.axis_size("batch")
    rank = lax.axis_index("tensor")
    rows, width = layer_input.shape
    hw = w_query.shape[1]
    fw = w_in.shape[1]
    lengths = doc_lengths[0]

    wqkv = jnp.concatenate([w_query, w_key, w_value], 1)
    bqkv = jnp.concatenate([query_bias, jnp.zeros_like(query_bias), value_bias]).astype(F32)
    tail_row = jnp.concatenate([inner_gain, inner_shift, jnp.zeros((fw - 2 * hw,), BF16)])
    sm = jnp.stack([in_bias, hidden_gain, hidden_shift, tail_row] + [tail_row] * 12)
    vec1 = jnp.stack([first_gain, first_shift] * 8)
    vec2 = jnp.stack([proj_bias, second_gain, second_shift, out_bias] * 4)

    qkv, normed_t, *gathered = front(
        layer_input, vec1, wqkv, bqkv[None], w_in, w_out, w_proj, sm, nt
    )
    heads, lse = attn_fwd(lengths, qkv, 512, 512)
    layer_output, mixed_grad, heads_grad, ra, rb, vsum, fsum = middle(
        heads, layer_input, cotangent, (w_in, w_out, w_proj, sm), gathered, vec2, ROWS, nt
    )

    bbits = bits_of(nb)
    ra0 = (ra[0].astype(F32) + swapped(ra[1], "tensor", 2).astype(F32)).astype(BF16)
    split = (2,) * len(bbits)
    rb = halve(rb.reshape((2,) + split + (width // nb, fw)), len(bbits), "batch", 1)
    ra0 = halve(ra0.reshape(split + (width // nb, fw + hw)), len(bbits) - 1, "batch", 1)
    rb0 = (rb[0].astype(F32) + swapped(rb[1], "tensor", 2).astype(F32)).astype(BF16)
    for i, bit in enumerate(bbits[1:]):
        dim = len(bbits) - 2 - i
        ra0 = halve(ra0, dim, "batch", bit)
        rb0 = halve(rb0, dim, "batch", bit)
    ra0 = ra0.astype(F32)
    rb0 = rb0.astype(F32)

    dqkv = attn_bwd(lengths, qkv, heads, heads_grad, lse, 512, 512)
    input_grad, g_qkv, first_sums, bias_sums = tail(
        dqkv, normed_t, wqkv, layer_input, mixed_grad, vec1, nt, nb
    )

    def placed(piece):
        return lax.dynamic_update_slice(
            jnp.zeros((nt * piece.shape[0],), F32), piece, (rank * piece.shape[0],)
        )

    def ordered(blocks):
        return jnp.concatenate(
            [lax.dynamic_index_in_dim(blocks, r ^ rank, 0, keepdims=False) for r in range(nt)]
        )

    full = [
        first_sums[0],
        first_sums[1],
        placed(bias_sums[0, :hw]),
        placed(bias_sums[0, 2 * hw :]),
        ordered(vsum[0].reshape(nt, hw)),
        ordered(vsum[1].reshape(nt, hw)),
        vsum[2],
        vsum[3],
        vsum[4],
        ordered(fsum[:, 0]),
        ordered(fsum[:, 1]),
        ordered(fsum[:, 2]),
        vsum[5],
    ]
    ndev = nb * nt
    packed = jnp.concatenate([v.reshape(ndev, -1) for v in full], 1)
    length = packed.shape[1]
    high = -(-length // 1024) * 8
    packed = jnp.pad(packed, ((0, 0), (0, high * 128 - length)))
    packed = vector_sums(packed.reshape(nb, nt, high, 128)).reshape(-1)
    vectors = []
    at = 0
    for v in full:
        size = v.shape[0] // ndev
        vectors.append(packed[at : at + size])
        at += size

    return (
        layer_output,
        input_grad,
        vectors[0],
        vectors[1],
        g_qkv[:, :hw],
        g_qkv[:, hw : 2 * hw],
        g_qkv[:, 2 * hw :],
        vectors[2],
        vectors[3],
        vectors[4],
        vectors[5],
        ra0[:, fw:].T,
        vectors[6],
        vectors[7],
        vectors[8],
        ra0[:, :fw],
        vectors[9],
        vectors[10],
        vectors[11],
        rb0.T,
        vectors[12],
    )


def solution(mesh):
    both = ("batch", "tensor")
    in_specs = (
        P(both, None),
        P("batch", None),
        P(),
        P(),
        P(None, "tensor"),
        P(None, "tensor"),
        P(None, "tensor"),
        P("tensor"),
        P("tensor"),
        P("tensor"),
        P("tensor"),
        P("tensor", None),
        P(),
        P(),
        P(),
        P(None, "tensor"),
        P("tensor"),
        P("tensor"),
        P("tensor"),
        P("tensor", None),
        P(),
        P(both, None),
    )
    vector = P(both)
    out_specs = (
        P(both, None),
        P(both, None),
        vector,
        vector,
        P("batch", "tensor"),
        P("batch", "tensor"),
        P("batch", "tensor"),
        vector,
        vector,
        vector,
        vector,
        P("tensor", "batch"),
        vector,
        vector,
        vector,
        P("batch", "tensor"),
        vector,
        vector,
        vector,
        P("tensor", "batch"),
        vector,
    )
    return jax.shard_map(body, mesh=mesh, in_specs=in_specs, out_specs=out_specs, check_vma=False)
```

```python
import functools
import math

import jax
import jax.numpy as jnp
from jax import lax
from jax.experimental import pallas as pl
from jax.experimental.pallas import tpu as pltpu
from jax.sharding import PartitionSpec as P

HDIM = 64
SLOT = 128
TILE = 512
LONGEST = 2048
EPS = 1e-05
SCALE = 0.125
LOG2E = 1.4426950408889634
NEG = -1e30
F32 = jnp.float32
BF16 = jnp.bfloat16


def dot_nn(a, b):
    return jnp.dot(a, b, preferred_element_type=F32)


def dot_nt(a, b):
    return lax.dot_general(a, b, (((1,), (1,)), ((), ())), preferred_element_type=F32)


def doc_ends(len_ref):
    ends = []
    total = jnp.int32(0)
    for i in range(len_ref.shape[0]):
        total = total + len_ref[i]
        ends.append(total)
    return ends


def halves_of(n):
    cut = next(i for i in range(1, n + 1) if 2 * i * (i + 1) >= n * (n + 1) - 2 * n)
    return [list(range(cut)), list(range(cut, n))]


def doc_lanes(len_ref, first, rows):
    ends = doc_ends(len_ref)
    lane = lax.broadcasted_iota(jnp.int32, (1, SLOT - HDIM), 1)
    low = jnp.zeros((1, SLOT - HDIM), jnp.int32)
    high = jnp.zeros((1, SLOT - HDIM), jnp.int32)
    for i, end in enumerate(ends):
        low = jnp.where(lane == i, end - len_ref[i], low)
        high = jnp.where(lane == i, end, high)
    pos = first + lax.broadcasted_iota(jnp.int32, (rows, 1), 0)
    return (pos >= low) & (pos < high)


def reaches(i, j):
    return (i - j) * TILE - (TILE - 1) < LONGEST


def causal(s):
    key = lax.broadcasted_iota(jnp.int32, s.shape, 0)
    query = lax.broadcasted_iota(jnp.int32, s.shape, 1)
    return jnp.where(key <= query, s, NEG)


def blk(i):
    return slice(i * TILE, (i + 1) * TILE)


def forward_tiles(h, blocks, qa_ref, ka_ref, vt_s, out_ref, lse_ref):
    at = slice(h * HDIM, (h + 1) * HDIM)
    for i in blocks:
        query = qa_ref[h, blk(i), :]
        peak = jnp.full((1, TILE), NEG, F32)
        acc = jnp.zeros((HDIM + 16, TILE), F32)
        for j in range(i + 1):
            if not reaches(i, j):
                continue
            s = dot_nt(ka_ref[h, blk(j), :], query)
            if i == j:
                s = causal(s)
            new = jnp.maximum(peak, jnp.max(s, 0, keepdims=True) * (SCALE * LOG2E))
            p = jnp.exp2(s * (SCALE * LOG2E) - new).astype(BF16)
            acc = acc * jnp.exp2(peak - new) + dot_nn(vt_s[h, : HDIM + 16, blk(j)], p)
            peak = new
        total = acc[HDIM : HDIM + 1]
        out_ref[at, blk(i)] = (acc[:HDIM] / total).astype(BF16)
        lse_ref[h : h + 1, blk(i)] = peak + jnp.log2(total)


MESH = pl.DeviceIdType.MESH
ROWS = 256


def flip1(i):
    return i + 1 - 2 * (i % 2)


def flip2(i):
    return i + 2 - 4 * ((i // 2) % 2)


def flips(t):
    return [t, flip1(t), flip2(t), flip1(flip2(t))]


def flip_bit(i, bit):
    return i + bit - 2 * bit * ((i // bit) % 2)


def greet(partners):
    barrier = pltpu.get_barrier_semaphore()
    for p in partners:
        pl.semaphore_signal(barrier, inc=1, device_id=p, device_id_type=MESH)
    pl.semaphore_wait(barrier, len(partners))


def copier(send, recv):
    def copy(src, dst, i, dev):
        return pltpu.make_async_remote_copy(
            src_ref=src,
            dst_ref=dst,
            send_sem=send.at[i],
            recv_sem=recv.at[i],
            device_id=dev,
            device_id_type=MESH,
        )

    return copy


def bits_of(n):
    return [1 << i for i in range(n.bit_length() - 1)]


def ln_stats(v, n):
    mean = jnp.sum(v, -1, keepdims=True) * (1.0 / n)
    var = jnp.sum(v * v, -1, keepdims=True) * (1.0 / n) - mean * mean
    return mean, lax.rsqrt(var + EPS)


def ln_back(dh, hat, inv, n):
    m0 = jnp.sum(dh, -1, keepdims=True) * (1.0 / n)
    m1 = jnp.sum(dh * hat, -1, keepdims=True) * (1.0 / n)
    return inv * (dh - m0 - hat * m1)


def col_sum(v):
    return jnp.sum(v, 0, keepdims=True)


def front_kernel(
    nh,
    len_ref, x_ref, sm_ref, wq_ref, wk_ref, wv_ref, wi_ref, wo_ref, wp_ref,
    qa_ref, ka_ref, va_ref, kt_ref, nt_ref, out_ref, lse_ref, wi_all, wo_all, wp_all, sm_all,
    nrm, w_s, qa_s, ka_s, va_s, kt_s, nt_s, vt_s, send, recv, local,
):
    b = lax.axis_index("batch")
    t = lax.axis_index("tensor")
    ranks = flips(t)
    core, across = (b, ranks[1]), (b, ranks[2])
    side, near = (flip1(b), t), (flip2(b), t)
    rows, full_width = x_ref.shape
    chunks = rows // ROWS
    width = nh * HDIM
    copy = copier(send, recv)
    greet([core, across, side, near])

    weights = [(wi_ref, wi_all), (wo_ref, wo_all), (wp_ref, wp_all)]
    order = [2, 0, 1]
    quarter = b % 4
    parts = [quarter, flip1(quarter), flip2(quarter), flip1(flip2(quarter))]

    def part(a, ref, q):
        depth = weights[a][0].shape[0] // 4
        return ref.at[pl.ds(pl.multiple_of(parts[q] * depth, depth), depth)]

    sends = []

    def go(c):
        c.start()
        sends.append(c)
        return c

    gain = sm_ref[4:5, :].astype(F32)
    shift = sm_ref[5:6, :].astype(F32)

    def chunk(j, k):
        return nrm.at[j, pl.ds(k * ROWS, ROWS)]

    near_by = []
    far = []
    for k in range(chunks):
        v = x_ref[k * ROWS : (k + 1) * ROWS, :].astype(F32)
        mean, inv = ln_stats(v, full_width)
        nrm[0, k * ROWS : (k + 1) * ROWS, :] = ((v - mean) * inv * gain + shift).astype(BF16)
        far.append(go(copy(chunk(0, k), chunk(2, k), 8 + chunks + k, across)))
        near_by.append(go(copy(chunk(0, k), chunk(1, k), 8 + k, core)))
    base = 8 + 3 * chunks
    whole = []
    for a in order:
        src, dst = weights[a]
        whole.append(go(copy(src, dst.at[0], 4 + a, core)))
    whole.append(go(copy(sm_ref, sm_all.at[0], 7, core)))

    for i, ref in enumerate((wq_ref, wk_ref, wv_ref)):
        w_s[i * width : (i + 1) * width, :] = ref[...]
    nt_s[full_width:, :] = jnp.ones((16, nt_s.shape[1]), BF16)
    biases = sm_ref[10:11, :].astype(F32)
    bias = jnp.concatenate(
        [biases[:, :width], jnp.zeros((1, width), F32), biases[:, width : 2 * width]], 1
    )
    lane = lax.broadcasted_iota(jnp.int32, (ROWS, SLOT - HDIM), 1)
    ones = jnp.where(lane < 16, 1.0, 0.0).astype(BF16)

    def project(j, k):
        first = pl.multiple_of(ranks[j] * rows + k * ROWS, ROWS)
        at = pl.ds(first, ROWS)
        low = nrm[j, k * ROWS : (k + 1) * ROWS, :]
        val = (dot_nt(low, w_s[...]) + bias).astype(BF16)
        nt_s[:full_width, at] = low.T
        inside = doc_lanes(len_ref, first, ROWS)
        member = inside.astype(F32).astype(BF16)
        outside = jnp.where(inside | (lane >= len_ref.shape[0]), 0.0, NEG).astype(BF16)
        for h in range(nh):
            q, k_, v = [val[:, c * width + h * HDIM : c * width + (h + 1) * HDIM] for c in range(3)]
            qa_s[h, at, :] = jnp.concatenate([q, outside], 1)
            keys = jnp.concatenate([k_, member], 1)
            ka_s[h, at, :] = keys
            kt_s[h, :, at] = keys.T[:HDIM]
            vals = jnp.concatenate([v, ones], 1)
            va_s[h, at, :] = vals
            vt_s[h, :, at] = vals.T[: HDIM + 16]

    def from_across(a):
        first[a].wait_recv()
        ref = part(a, weights[a][1].at[1], 0)
        go(copy(ref, ref, base + a, side))
        go(copy(ref, ref, base + 3 + a, near))
        to_core(a, 0)

    def to_core(a, q):
        ref = part(a, weights[a][1].at[1], q)
        go(copy(ref, part(a, weights[a][1].at[2], q), base + 9 + 4 * a + q, core))

    def from_sides(a):
        ref = part(a, weights[a][1].at[1], 1)
        copy(ref, ref, base + a, side).wait_recv()
        to_core(a, 1)
        ref = part(a, weights[a][1].at[1], 2)
        copy(ref, ref, base + 3 + a, near).wait_recv()
        to_core(a, 2)

    def from_across_last(a):
        last[a].wait_recv()
        to_core(a, 3)

    for k in range(chunks):
        project(0, k)
    for k in range(chunks):
        near_by[k].wait_recv()
        project(1, k)
    first, last = {}, {}
    for k in range(chunks):
        far[k].wait_recv()
        go(copy(chunk(2, k), chunk(3, k), 8 + 2 * chunks + k, core))
        if k == chunks - 1:
            small_x = go(copy(sm_ref, sm_all.at[1], 3, across))
            for a in order:
                src, dst = weights[a]
                first[a] = go(copy(part(a, src, 0), part(a, dst.at[1], 0), a, across))
            for a in order:
                src, dst = weights[a]
                last[a] = go(copy(part(a, src, 3), part(a, dst.at[1], 3), base + 6 + a, across))
        project(2, k)
    for k in range(chunks):
        copy(chunk(2, k), chunk(3, k), 8 + 2 * chunks + k, core).wait_recv()
        project(3, k)
    kept = [(qa_s, qa_ref), (ka_s, ka_ref), (va_s, va_ref), (kt_s, kt_ref), (nt_s, nt_ref)]
    stores = [pltpu.make_async_copy(s, d, local.at[i]) for i, (s, d) in enumerate(kept)]
    for c in stores:
        c.start()

    def small_on():
        small_x.wait_recv()
        go(copy(sm_all.at[1], sm_all.at[2], base + 21, core))

    steps = [
        [lambda: from_across(2), small_on],
        [lambda: from_across(0)],
        [lambda: from_across(1)],
        [lambda: from_sides(2), lambda: from_sides(0)],
        [lambda: from_sides(1), lambda: from_across_last(2)],
        [lambda: from_across_last(0), lambda: from_across_last(1)],
    ]
    for h in range(nh):
        for blocks in halves_of(qa_s.shape[1] // TILE):
            forward_tiles(h, blocks, qa_s, ka_s, vt_s, out_ref, lse_ref)
            if steps:
                for f in steps.pop(0):
                    f()
    for rest in steps:
        for f in rest:
            f()
    copy(sm_all.at[1], sm_all.at[2], base + 21, core).wait_recv()
    for c in whole:
        c.wait_recv()
    for a in order:
        for q in range(4):
            ref = part(a, weights[a][1].at[2], q)
            copy(ref, ref, base + 9 + 4 * a + q, core).wait_recv()
    for c in sends:
        c.wait_send()
    for c in stores:
        c.wait()


def front(lengths, x, sm, wq, wk, wv, wi, wo, wp, nt):
    rows, width = x.shape
    group = rows * nt
    nh = wq.shape[0] // HDIM
    sems = 8 + 3 * (rows // ROWS) + 22
    vmem = pl.BlockSpec(memory_space=pltpu.VMEM)
    hbm = pl.BlockSpec(memory_space=pl.ANY)
    smem = pl.BlockSpec(memory_space=pltpu.SMEM)
    shape = jax.ShapeDtypeStruct
    slots = (nh, group, SLOT)
    return pl.pallas_call(
        functools.partial(front_kernel, nh),
        out_shape=(
            shape(slots, BF16),
            shape(slots, BF16),
            shape(slots, BF16),
            shape((nh, HDIM, group), BF16),
            shape((width + 16, group), BF16),
            shape((nh * HDIM, group), BF16),
            shape((nh, group), F32),
            shape((nt - 1,) + wi.shape, BF16),
            shape((nt - 1,) + wo.shape, BF16),
            shape((nt - 1,) + wp.shape, BF16),
            shape((nt - 1,) + sm.shape, BF16),
        ),
        in_specs=[smem] + [vmem] * 5 + [hbm] * 3,
        out_specs=(hbm,) * 5 + (vmem,) * 2 + (hbm,) * 4,
        scratch_shapes=[
            pltpu.VMEM((nt, rows, width), BF16),
            pltpu.VMEM((3 * nh * HDIM, width), BF16),
            pltpu.VMEM(slots, BF16),
            pltpu.VMEM(slots, BF16),
            pltpu.VMEM(slots, BF16),
            pltpu.VMEM((nh, HDIM, group), BF16),
            pltpu.VMEM((width + 16, group), BF16),
            pltpu.VMEM((nh, HDIM + 16, group), BF16),
            pltpu.SemaphoreType.DMA((sems,)),
            pltpu.SemaphoreType.DMA((sems,)),
            pltpu.SemaphoreType.DMA((5,)),
        ],
        compiler_params=pltpu.CompilerParams(
            collective_id=0, has_side_effects=True, vmem_limit_bytes=56 << 20
        ),
        cost_estimate=pl.CostEstimate(
            flops=6 * group * width * nh * HDIM, bytes_accessed=20 << 20, transcendentals=0
        ),
        name="front",
    )(lengths, x, sm, wq, wk, wv, wi, wo, wp)


def mid_kernel(
    tm, nt,
    heads_ref, resid_ref, cot_ref, wi_own, wo_own, wp_own, wi_all, wo_all, wp_all,
    sm_own, sm_all,
    lout_ref, mg_ref, hg_all, o1_ref, o2_ref, o3_ref, vs_ref, is_ref, fs_ref,
    wi_s, wo_s, wp_s, hr_s, hg_s, act_s, dact_s, dh_s, hid_s, pre_s, inner_s,
    sec_t, cot_t, att_t, g1, g2, g3, r1, r2, r3, send, recv, local,
):
    b = lax.axis_index("batch")
    t = lax.axis_index("tensor")
    ranks = flips(t)
    devs = [(b, r) for r in ranks]
    step = pl.program_id(0)
    tiles = pl.num_programs(0) - nt
    n_tiles = hr_s.shape[2] // tm
    rows = n_tiles * tm
    width = resid_ref.shape[1]
    fw = wi_s.shape[2]
    ff = nt * fw
    hw = width // nt
    copy = copier(send, recv)

    def sm_row(j, i):
        ref = sm_own if j == 0 else sm_all.at[j - 1]
        return ref[i : i + 1, :].astype(F32)

    def lanes(rank, r):
        return pl.ds(pl.multiple_of(rank * rows + r * tm, tm), tm)

    def heads_in(j, r):
        return copy(
            heads_ref.at[:, lanes(ranks[j], r)],
            hr_s.at[j, :, pl.ds(pl.multiple_of(r * tm, tm), tm)],
            j * n_tiles + r,
            devs[j],
        )

    def own_heads():
        return pltpu.make_async_copy(
            heads_ref.at[:, pl.ds(pl.multiple_of(t * rows, tm), rows)], hr_s.at[0], local.at[6]
        )

    def grads_out(j, r):
        return copy(
            hg_s.at[j, :, pl.ds(pl.multiple_of(r * tm, tm), tm)],
            hg_all.at[:, lanes(t, r)],
            (nt + j) * n_tiles + r,
            devs[j],
        )

    def own_grads():
        return pltpu.make_async_copy(
            hg_s.at[0], hg_all.at[:, pl.ds(pl.multiple_of(t * rows, tm), rows)], local.at[7]
        )

    base = 2 * nt * n_tiles
    cut = g1.shape[2]

    given, taken, outs = [g1, g2, g3], [r1, r2, r3], [o1_ref, o2_ref, o3_ref]

    def pair_sum(i, s):
        return copy(given[i].at[s], taken[i].at[s], base + 2 * i + s, devs[1])

    def put(i, s):
        return pltpu.make_async_copy(taken[i].at[s], outs[i].at[s], local.at[2 * i + s])

    def loads(own, rest, dst, i):
        return [
            pltpu.make_async_copy(own, dst.at[0], local.at[8 + 2 * i]),
            pltpu.make_async_copy(rest, dst.at[pl.ds(1, nt - 1)], local.at[9 + 2 * i]),
        ]

    load_p = loads(wp_own, wp_all, wp_s, 0)
    load_i = loads(wi_own, wi_all, wi_s, 1)
    load_o = loads(wo_own, wo_all, wo_s, 2)

    @pl.when(step == 0)
    def _():
        for c in load_p + load_i + load_o:
            c.start()
        own_heads().start()
        greet(devs[1:])
        for r in range(n_tiles):
            for j in (2, 3, 1):
                heads_in(j, r).start()
        vs_ref[...] = jnp.zeros_like(vs_ref)
        is_ref[...] = jnp.zeros_like(is_ref)
        fs_ref[...] = jnp.zeros_like(fs_ref)
        for c in load_p:
            c.wait()
        own_heads().wait()

    @pl.when(step < tiles)
    def _():
        r0 = pl.multiple_of(step * tm, tm)
        here = pl.ds(r0, tm)
        for j in range(1, nt):
            heads_in(j, step).wait_recv()
        proj_bias, second_gain, second_shift, out_bias = [sm_row(0, i) for i in range(6, 10)]
        tails = [sm_row(j, 3) for j in range(nt)]
        inner_gain = jnp.concatenate([v[:, :hw] for v in tails], 1)
        inner_shift = jnp.concatenate([v[:, hw : 2 * hw] for v in tails], 1)
        heads_t = jnp.concatenate([hr_s[j, :, here] for j in range(nt)], 0)
        heads = heads_t.T.astype(F32)
        mean, inner_inv = ln_stats(heads, width)
        inner_hat = (heads - mean) * inner_inv
        inner_low = (inner_hat * inner_gain + inner_shift).astype(BF16)
        for j in range(nt):
            inner_s[j, here, :] = inner_low[:, j * hw : (j + 1) * hw]
        wp = jnp.concatenate([wp_s[j] for j in range(nt)], 0)
        mixed = resid_ref[...].astype(F32) + (dot_nn(inner_low, wp) + proj_bias)
        mean, second_inv = ln_stats(mixed, width)
        second_hat = (mixed - mean) * second_inv
        second_low = (second_hat * second_gain + second_shift).astype(BF16)
        sec_t[:, here] = second_low.T
        cot_low = cot_ref[...]
        cot_t[:, here] = cot_low.T
        cot = cot_low.astype(F32)

        @pl.when(step == 0)
        def _():
            for c in load_i:
                c.wait()

        c0 = math.sqrt(2.0 / math.pi)
        c1 = 0.044715
        s0 = jnp.zeros((tm, 1), F32)
        s1 = jnp.zeros((tm, 1), F32)
        for j in range(nt):
            v = dot_nn(second_low, wi_s[j]) + sm_row(j, 0)
            v2 = v * v
            th = jnp.tanh(v * (c0 + (c0 * c1) * v2))
            half = 0.5 + 0.5 * th
            act = v * half
            dact = half + (0.5 * v) * (1.0 - th * th) * (c0 + (3.0 * c0 * c1) * v2)
            act_s[j] = act
            dact_s[j] = dact
            s0 += jnp.sum(act, -1, keepdims=True)
            s1 += jnp.sum(act * act, -1, keepdims=True)
        mean = s0 * (1.0 / ff)
        inv = lax.rsqrt(s1 * (1.0 / ff) - mean * mean + EPS)
        result = mixed + out_bias
        m0 = jnp.zeros((tm, 1), F32)
        m1 = jnp.zeros((tm, 1), F32)

        @pl.when(step == 0)
        def _():
            for c in load_o:
                c.wait()

        for j in range(nt):
            gain = sm_row(j, 1)
            hat = (act_s[j] - mean) * inv
            act_s[j] = hat
            hid = (hat * gain + sm_row(j, 2)).astype(BF16)
            hid_s[j, here, :] = hid
            result += dot_nn(hid, wo_s[j])
            gh = dot_nt(cot_low, wo_s[j])
            gn = gh * hat
            fs_ref[j, 1:2, :] += col_sum(gn)
            fs_ref[j, 2:3, :] += col_sum(gh)
            dh = gh * gain
            dh_s[j] = dh
            m0 += jnp.sum(dh, -1, keepdims=True)
            m1 += jnp.sum(gn * gain, -1, keepdims=True)
        lout_ref[...] = result.astype(BF16)
        m0 = m0 * (1.0 / ff)
        m1 = m1 * (1.0 / ff)
        second_grad = jnp.zeros((tm, width), F32)
        for j in range(nt):
            pre = (inv * (dh_s[j] - m0 - act_s[j] * m1) * dact_s[j]).astype(BF16)
            pre_s[j, here, :] = pre
            fs_ref[j, 0:1, :] += col_sum(pre.astype(F32))
            second_grad += dot_nt(pre, wi_s[j])
        vs_ref[3:4, :] += col_sum(second_grad * second_hat)
        vs_ref[4:5, :] += col_sum(second_grad)
        vs_ref[5:6, :] += col_sum(cot)
        mixed_grad = cot + ln_back(second_grad * second_gain, second_hat, second_inv, width)
        mg_ref[...] = mixed_grad
        vs_ref[2:3, :] += col_sum(mixed_grad)
        att = mixed_grad.astype(BF16)
        att_t[:, here] = att.T
        grad_inner = dot_nt(att, wp)
        gain_sum = col_sum(grad_inner * inner_hat)
        shift_sum = col_sum(grad_inner)
        for j in range(nt):
            is_ref[j, 0:1, :] += gain_sum[:, j * hw : (j + 1) * hw]
            is_ref[j, 1:2, :] += shift_sum[:, j * hw : (j + 1) * hw]
        hg = ln_back(grad_inner * inner_gain, inner_hat, inner_inv, width).astype(BF16).T
        prod = hg.astype(F32) * heads_t.astype(F32)
        row = lax.broadcasted_iota(jnp.int32, (16, 1), 0)
        for j in range(nt):
            hg_s[j, :hw, here] = hg[j * hw : (j + 1) * hw, :]
            below = jnp.zeros((16, tm), F32)
            for h in range(hw // HDIM):
                delta = -col_sum(prod[j * hw + h * HDIM : j * hw + (h + 1) * HDIM, :])
                high = delta.astype(BF16).astype(F32)
                below = jnp.where(row == 2 * h, high, below)
                below = jnp.where(row == 2 * h + 1, delta - high, below)
            hg_s[j, hw:, here] = below.astype(BF16)
        for j in (2, 3, 1):
            grads_out(j, step).start()

    @pl.when(step == tiles)
    def _():
        own_grads().start()

    @pl.when((step >= tiles) & (step < tiles + 2))
    def _():
        s = step - tiles
        j = 2 * s + 1
        gi = dot_nn(sec_t[...], pre_s[j]).astype(BF16)
        g1[s] = gi[:, :cut]
        pair_sum(0, s).start()
        go = dot_nn(cot_t[...], hid_s[j]).astype(BF16)
        g2[s] = go[:, :cut]
        pair_sum(1, s).start()
        gp = dot_nn(att_t[...], inner_s[j]).astype(BF16)
        g3[s] = jnp.concatenate([gi[:, cut:], go[:, cut:], gp], 1)
        pair_sum(2, s).start()

    @pl.when(step >= tiles + 2)
    def _():
        s = step - tiles - 2
        j = 2 * s
        def add(i, mine):
            pair_sum(i, s).wait_recv()
            taken[i][s] = (mine + taken[i][s].astype(F32)).astype(BF16)
            put(i, s).start()

        gi = dot_nn(sec_t[...], pre_s[j])
        add(0, gi[:, :cut])
        go = dot_nn(cot_t[...], hid_s[j])
        add(1, go[:, :cut])
        gp = dot_nn(att_t[...], inner_s[j])
        add(2, jnp.concatenate([gi[:, cut:], go[:, cut:], gp], 1))

    @pl.when(step == pl.num_programs(0) - 1)
    def _():
        own_grads().wait()
        for r in range(n_tiles):
            for j in range(1, nt):
                heads_in(j, r).wait_send()
                grads_out(j, r).wait_send()
                grads_out(j, r).wait_recv()
        for i in range(3):
            for s in range(2):
                pair_sum(i, s).wait_send()
                put(i, s).wait()


def middle(heads, resid, cot, own, gathered, tm, nt):
    wi, wo, wp, sm = own
    hw, group = heads.shape
    rows, width = resid.shape
    fw = wi.shape[1]
    tiles = rows // tm
    last = tiles - 1
    tile = lambda i: jnp.minimum(i, last)
    hbm = pl.BlockSpec(memory_space=pl.ANY)
    vmem = pl.BlockSpec(memory_space=pltpu.VMEM)
    shape = jax.ShapeDtypeStruct
    block = pl.BlockSpec((tm, width), lambda i: (tile(i), 0))
    sems = 2 * nt * tiles + 6
    cut = fw - SLOT
    widths = [cut, cut, 2 * SLOT + hw]
    return pl.pallas_call(
        functools.partial(mid_kernel, tm, nt),
        out_shape=(
            shape((rows, width), BF16),
            shape((rows, width), F32),
            shape((hw + 16, group), BF16),
        )
        + tuple(shape((2, width, n), BF16) for n in widths)
        + (
            shape((8, width), F32),
            shape((nt, 8, hw), F32),
            shape((nt, 8, fw), F32),
        ),
        grid=(tiles + nt,),
        in_specs=[hbm, block, block] + [hbm] * 6 + [vmem] * 2,
        out_specs=(block, block) + (hbm,) * 4 + (vmem,) * 3,
        scratch_shapes=[
            pltpu.VMEM((nt,) + wi.shape, BF16),
            pltpu.VMEM((nt,) + wo.shape, BF16),
            pltpu.VMEM((nt,) + wp.shape, BF16),
            pltpu.VMEM((nt, hw, rows), BF16),
            pltpu.VMEM((nt, hw + 16, rows), BF16),
            pltpu.VMEM((nt, tm, fw), F32),
            pltpu.VMEM((nt, tm, fw), F32),
            pltpu.VMEM((nt, tm, fw), F32),
            pltpu.VMEM((nt, rows, fw), BF16),
            pltpu.VMEM((nt, rows, fw), BF16),
            pltpu.VMEM((nt, rows, hw), BF16),
            pltpu.VMEM((width, rows), BF16),
            pltpu.VMEM((width, rows), BF16),
            pltpu.VMEM((width, rows), BF16),
        ]
        + [pltpu.VMEM((2, width, n), BF16) for n in widths * 2]
        + [
            pltpu.SemaphoreType.DMA((sems,)),
            pltpu.SemaphoreType.DMA((sems,)),
            pltpu.SemaphoreType.DMA((14,)),
        ],
        compiler_params=pltpu.CompilerParams(
            collective_id=1, has_side_effects=True, vmem_limit_bytes=62 << 20
        ),
        cost_estimate=pl.CostEstimate(
            flops=12 * nt * rows * width * fw + 6 * rows * width * width,
            bytes_accessed=30 << 20,
            transcendentals=nt * rows * fw,
        ),
        name="middle",
    )(heads, resid, cot, wi, wo, wp, *gathered[:3], sm, gathered[3])


class Chain:
    def __init__(self, hops, source, came, kept, base, copy, local):
        self.hops, self.source, self.came, self.kept = hops, source, came, kept
        self.base, self.copy, self.local = base, copy, local
        self.at = 0

    def select(self, m, mine):
        kind, bit, _ = self.hops[m]
        buf = self.source if m == 0 else self.kept[m - 1]
        if kind == "x":
            return buf.at[pl.ds(0 if mine else 1, 1)]
        return buf.at[:, :, bit if mine else 1 - bit]

    def swap(self, m):
        return self.copy(self.select(m, False), self.came[m], self.base + m, self.hops[m][2])

    def loads(self):
        kind = self.hops[0][0]
        src = self.select(0, True)
        if kind != "b":
            return [pltpu.make_async_copy(src, self.kept[0], self.local.at[0])]
        return [
            pltpu.make_async_copy(src.at[:, i], self.kept[0].at[:, i // 2, i % 2], self.local.at[i])
            for i in range(src.shape[1])
        ]

    def start(self):
        self.swap(0).start()
        if self.local is not None:
            for c in self.loads():
                c.start()

    def advance(self):
        m = self.at
        self.at += 1
        kind = self.hops[m][0]
        last = m == len(self.hops) - 1
        self.swap(m).wait_recv()
        came = self.came[m]
        if m == 0 and self.local is not None:
            for c in self.loads():
                c.wait()
        if kind == "b":
            n = came.shape[1]
            for i in range(n):
                at = (slice(None), i // 2, i % 2) if n > 1 else (slice(None), 0, 0)
                if m == 0 and self.local is not None:
                    mine = self.kept[0][at]
                else:
                    mine = self.select(m, True)[:, i]
                total = mine.astype(F32) + came[:, i].astype(F32)
                if last:
                    return total
                self.kept[m][at] = total.astype(BF16)
        else:
            if m == 0 and self.local is not None:
                mine = self.kept[0][...]
            else:
                mine = self.select(m, True)[...]
            total = mine.astype(F32) + came[...].astype(F32)
            if last:
                return total[0, 0]
            self.kept[m][...] = total.astype(BF16)
        self.swap(m + 1).start()
        return None

    def finish(self):
        for m in range(len(self.hops)):
            self.swap(m).wait_send()


def chain_shapes(kinds, nb, rows, cols):
    wide = 2 if any(k[0] == "x" for k in kinds) else 1
    n = nb // 2
    tail = (rows, cols)
    source = (wide, n // 2, 2, 2) + tail if kinds[0][0] == "c" else (wide, n, 2) + tail
    came, kept = [], []
    for kind, _ in kinds:
        if kind == "c":
            n //= 2
            came.append((wide, n, 2) + tail)
            kept.append((wide, n, 2) + tail)
        elif kind == "x":
            wide = 1
            came.append((wide, n, 2) + tail)
            kept.append((wide, n, 2) + tail)
        else:
            came.append((wide, n) + tail)
            n //= 2
            kept.append((wide, max(n, 1), 2) + tail)
    return source, came, kept[:-1]


def group_list(n):
    left = list(range(n))
    groups = []
    while left:
        if len(groups) % 2 == 0:
            g = left.pop()
            groups.append((g, [(g, j) for j in left + [g] if reaches(g, j)]))
        else:
            g = left.pop(0)
            groups.append((g, [(i, g) for i in [g] + left if reaches(i, g)]))
    return groups


def chain_kinds(nb, nh):
    bits = list(range(nb.bit_length() - 1))
    hops = [("b", i) for i in bits]
    x = [("x", None)]
    return [
        x + hops,
        hops[:2] + x + hops[2:],
        [("c", 1)] + x + hops[:1] + hops[2:],
    ] + [hops] * (nh - 1)


def back_kernel(
    nt, nb, nh, kinds,
    qa_ref, ka_ref, va_ref, kt_ref, nt_ref, grad_ref, lse_ref, x_ref, mg_ref, sm_ref,
    wq_ref, wk_ref, wv_ref, s1_ref, s2_ref, s3_ref, vs_ref, is_ref, fs_ref,
    ig_ref, f1_ref, f2_ref, f3_ref, gq_ref, e_ref,
    qa_s, ka_s, va_s, kt_s, nt_s, g_s, dl_s, wh_s, dq_s, dk_s, dv_s, d_s,
    part_s, core_r, far_r, last_s, last_r, e_s, e1_r, sum1_s, e2_r, sum2_s,
    send, recv, local, *rest,
):
    b = lax.axis_index("batch")
    t = lax.axis_index("tensor")
    ranks = flips(t)
    core, across = (b, ranks[1]), (b, ranks[2])
    group = [(b, r) for r in ranks]
    everyone = [((b + i) % nb, t) for i in range(nb)]
    bits = bits_of(nb)
    rows, width = x_ref.shape
    chunks = rows // ROWS
    total_rows = qa_s.shape[1]
    hw = nh * HDIM
    depth = width // nb
    copy = copier(send, recv)
    sems = [0]

    def take(n):
        sems[0] += n
        return sems[0] - n

    spots = [0]

    def fetch(src, dst):
        spots[0] += 1
        return pltpu.make_async_copy(src, dst, local.at[spots[0] - 1])

    load_head = []
    for h in range(nh):
        at = pl.ds(h * HDIM, HDIM)
        load_head.append(
            [fetch(r.at[h], s.at[h]) for r, s in ((qa_ref, qa_s), (ka_ref, ka_s), (va_ref, va_s), (kt_ref, kt_s))]
            + [fetch(grad_ref.at[at], g_s.at[h, pl.ds(0, HDIM)])]
        )
    load_delta = fetch(grad_ref.at[pl.ds(hw, 16)], dl_s)
    load_normed = fetch(nt_ref, nt_s)
    load_mixed = fetch(mg_ref, ig_ref)
    load_wh = [
        fetch(w.at[pl.ds(h * HDIM, HDIM)], wh_s.at[h, pl.ds(c * HDIM, HDIM)])
        for h in range(nh)
        for c, w in enumerate((wq_ref, wk_ref, wv_ref))
    ]
    for c in [load_delta] + load_head[0]:
        c.start()
    greet(group[1:] + everyone[1:])

    rest = list(rest)
    chains = []
    for i, kind in enumerate(kinds):
        source = [s1_ref, s2_ref, s3_ref][i] if i < 3 else rest.pop(0)
        came = [rest.pop(0) for _ in kind]
        kept = [rest.pop(0) for _ in kind[1:]]
        hops = [
            ("x", None, across)
            if k == "x"
            else (k, (b // bits[bit]) % 2, (flip_bit(b, bits[bit]), t))
            for k, bit in kind
        ]
        own = None
        if i < 3:
            n = nb // 2 if kind[0][0] == "b" else 1
            own = local.at[pl.ds(spots[0], n)]
            spots[0] += n
        chains.append(Chain(hops, source, came, kept, take(len(kind)), copy, own))
    weights, heads = chains[:3], chains[3:]
    for c in weights:
        c.start()
    for loads in load_head[1:] + [[load_normed], load_wh, [load_mixed]]:
        for c in loads:
            c.start()

    row = lax.broadcasted_iota(jnp.int32, (SLOT - HDIM, 1), 0)
    load_delta.wait()
    for h in range(nh):
        delta = dl_s[2 * h : 2 * h + 2, :].astype(F32)
        below = jnp.where(row == 0, delta[0:1], jnp.where(row == 1, delta[1:2], 0.0))
        g_s[h, HDIM:, :] = below.astype(BF16)

    def tile(h, i, j, query, grad):
        s = dot_nt(ka_s[h, blk(j), :], query)
        if i == j:
            s = causal(s)
        p = jnp.exp2(s * (SCALE * LOG2E) - lse_ref[h : h + 1, blk(i)])
        ds = (p * dot_nn(va_s[h, blk(j), :], g_s[h, :, blk(i)])).astype(BF16)
        return (
            dot_nn(kt_s[h, :, blk(j)], ds),
            dot_nn(ds, query[:, :HDIM]),
            dot_nn(p.astype(BF16), grad),
        )

    def sides(h, i):
        return qa_s[h, blk(i), :], g_s[h, :HDIM, blk(i)].T

    def run_group(h, g, pairs):
        if all(i == g for i, _ in pairs):
            query, grad = sides(h, g)
            acc = dq_s[:, blk(g)]
            for i, j in pairs:
                dq, dk, dv = tile(h, i, j, query, grad)
                acc += dq
                dk_s[blk(j), :] += dk
                dv_s[blk(j), :] += dv
            dq_s[:, blk(g)] = acc
        else:
            acc_k = dk_s[blk(g), :]
            acc_v = dv_s[blk(g), :]
            for i, j in pairs:
                dq, dk, dv = tile(h, i, j, *sides(h, i))
                dq_s[:, blk(i)] += dq
                acc_k += dk
                acc_v += dv
            dk_s[blk(g), :] = acc_k
            dv_s[blk(g), :] = acc_v
        d_s[h, blk(g), :] = jnp.concatenate(
            [(dq_s[:, blk(g)] * SCALE).T, dk_s[blk(g), :] * SCALE, dv_s[blk(g), :]], 1
        ).astype(BF16)

    def clear():
        dq_s[...] = jnp.zeros_like(dq_s)
        dk_s[...] = jnp.zeros_like(dk_s)
        dv_s[...] = jnp.zeros_like(dv_s)

    head_sums = []
    last_base = take(nb)

    def last_send(i):
        return copy(last_s.at[everyone[i][0]], last_r.at[i], last_base + i, everyone[i])

    def weight_part(h):
        grad = dot_nn(nt_s[...], d_s[h])
        head_sums.append(grad[width : width + 1])
        grad = grad.astype(BF16)
        for i in range(nb):
            piece = grad[i * depth : (i + 1) * depth, :]
            if h < nh - 1:
                heads[h].source[0, i // 2, i % 2] = piece
            else:
                last_s[i] = piece
        if h < nh - 1:
            heads[h].start()
        else:
            for i in range(1, nb):
                last_send(i).start()

    core_base = take(2 * chunks)
    far_base = take(chunks)

    def to_core(kind, k):
        return copy(
            part_s.at[2 * kind + 1, k], core_r.at[kind, k], core_base + kind * chunks + k, core
        )

    def to_far(k):
        return copy(part_s.at[2, k], far_r.at[k], far_base + k, across)

    def block_of(rank):
        return (rank + t) % 2 + 2 * ((rank // 2 + t // 2) % 2)

    def give(c):
        rank, k = c // chunks, c % chunks
        at = slice(c * ROWS, (c + 1) * ROWS)
        part = dot_nn(d_s[0, at, :], wh_s[0])
        for h in range(1, nh):
            part += dot_nn(d_s[h, at, :], wh_s[h])
        j = block_of(rank)
        part_s[j, k] = part.astype(BF16)

        @pl.when(j == 1)
        def _():
            to_core(0, k).start()

        @pl.when(j == 3)
        def _():
            to_core(1, k).start()

    def relay(c):
        rank, k = c // chunks, c % chunks

        @pl.when(block_of(rank) == 2)
        def _():
            to_core(1, k).wait_recv()
            part_s[2, k] = (part_s[2, k].astype(F32) + core_r[1, k].astype(F32)).astype(BF16)
            to_far(k).start()

    outs = [f1_ref, f2_ref, f3_ref] + [gq_ref.at[i] for i in range(nh - 1)]

    def step(c):
        if c.at < len(c.hops):
            done = c.advance()
            if done is not None:
                outs[chains.index(c)][...] = done[0]

    groups = group_list(total_rows // TILE)
    per = TILE // ROWS
    points = {
        (nh - 3, len(groups) - 1): weights,
        (nh - 2, 2): weights + heads[:1],
        (nh - 1, 1): weights + heads,
    }
    for h in range(nh):
        for c in load_head[h]:
            c.wait()
        clear()
        pending = []
        for n, (g, pairs) in enumerate(groups):
            run_group(h, g, pairs)
            if h == nh - 1:
                if n == 0:
                    for c in load_wh:
                        c.wait()
                for c in pending:
                    relay(c)
                pending = list(range(g * per, (g + 1) * per))
                for c in pending:
                    give(c)
            for c in points.get((h, n), []):
                step(c)
        if h == 0:
            load_normed.wait()
        weight_part(h)
    for c in pending:
        relay(c)
    for c in heads:
        step(c)

    gain = sm_ref[4:5, :].astype(F32)
    firsts = [jnp.zeros((1, width), F32), jnp.zeros((1, width), F32)]
    load_mixed.wait()
    for k in range(chunks):
        to_core(0, k).wait_recv()
        to_far(k).wait_recv()
        grad = part_s[0, k].astype(F32) + core_r[0, k].astype(F32) + far_r[k].astype(F32)
        at = slice(k * ROWS, (k + 1) * ROWS)
        v = x_ref[at, :].astype(F32)
        mean, inv = ln_stats(v, width)
        hat = (v - mean) * inv
        firsts[0] += col_sum(grad * hat)
        firsts[1] += col_sum(grad)
        ig_ref[at, :] += ln_back(grad * gain, hat, inv, width)

    query_sum = jnp.concatenate([s[:, :HDIM] for s in head_sums], 1)
    value_sum = jnp.concatenate([s[:, 2 * HDIM :] for s in head_sums], 1)
    nothing = jnp.zeros((1, width), F32)
    for r in range(nt):
        j = block_of(r)
        mine = jnp.where(j == 0, 1.0, 0.0)
        e_s[r, 0:3, :] = fs_ref[j, 0:3, :]
        inner = is_ref[j]
        e_s[r, 3:4, :] = jnp.concatenate(
            [inner[0:1], inner[1:2], query_sum * mine, value_sum * mine], 1
        )
        e_s[r, 4:5, :] = vs_ref[2 + r : 3 + r, :]
        e_s[r, 5:6, :] = firsts[r] if r < 2 else nothing
        e_s[r, 6:8, :] = jnp.zeros((2, width), F32)
    e_base = take(2 * nt + nb)

    def hop1(j):
        return copy(e_s.at[ranks[j]], e1_r.at[j], e_base + j, group[j])

    def hop2(i):
        return copy(sum1_s, e2_r.at[i], e_base + nt + i, everyone[i])

    def hop3(j):
        return copy(sum2_s, e_ref.at[t], e_base + nt + nb + j, group[j])

    def hop3_came(j):
        return copy(sum2_s, e_ref.at[ranks[j]], e_base + nt + nb + j, group[j])

    for j in range(1, nt):
        hop1(j).start()
    for c in weights + heads:
        step(c)
    total = e_s[t]
    for j in range(1, nt):
        hop1(j).wait_recv()
        total += e1_r[j]
    sum1_s[...] = total
    for i in range(1, nb):
        hop2(i).start()
    turns = max(len(c.hops) for c in chains)
    for _ in range(turns):
        for c in chains:
            step(c)
    last = last_s[b].astype(F32)
    for i in range(1, nb):
        last_send(i).wait_recv()
        last += last_r[i].astype(F32)
    gq_ref[nh - 1] = last
    for i in range(1, nb):
        hop2(i).wait_recv()
        total += e2_r[i]
    sum2_s[...] = total
    for j in range(1, nt):
        hop3(j).start()
    e_ref[t] = total
    for k in range(chunks):
        to_core(0, k).wait_send()
        to_core(1, k).wait_send()
        to_far(k).wait_send()
    for c in chains:
        c.finish()
    for i in range(1, nb):
        last_send(i).wait_send()
        hop2(i).wait_send()
    for j in range(1, nt):
        hop3_came(j).wait_recv()
        hop1(j).wait_send()
        hop3(j).wait_send()


def back(slots, normed_t, grad, lse, x, mixed_grad, sm, w3, sums, vecs, nt, nb):
    qa, ka, va, kt = slots
    rows, width = x.shape
    nh, group, _ = qa.shape
    hw = nh * HDIM
    cols = 3 * HDIM
    depth = width // nb
    chunks = rows // ROWS
    kinds = chain_kinds(nb, nh)
    widths = [s.shape[-1] for s in sums] + [cols] * (nh - 1)
    bufs = []
    sources = []
    for i, kind in enumerate(kinds):
        source, came, kept = chain_shapes(kind, nb, depth, widths[i])
        if i < 3:
            sources.append(sums[i].reshape(source))
        else:
            came = [source] + came
        bufs += [pltpu.VMEM(s, BF16) for s in came + kept]
    sems = sum(len(k) for k in kinds) + 3 * chunks + 2 * nb + 2 * nt
    spots = 5 * nh + 3 + 3 * nh + 2 + nb // 2
    shape = jax.ShapeDtypeStruct
    vmem = pl.BlockSpec(memory_space=pltpu.VMEM)
    hbm = pl.BlockSpec(memory_space=pl.ANY)
    chunked = (chunks, ROWS, width)
    small = pltpu.VMEM((8, width), F32)
    return pl.pallas_call(
        functools.partial(back_kernel, nt, nb, nh, kinds),
        out_shape=(
            shape((rows, width), F32),
            shape((depth, widths[0]), F32),
            shape((depth, widths[1]), F32),
            shape((depth, widths[2]), F32),
            shape((nh, depth, cols), F32),
            shape((nt, 8, width), F32),
        ),
        in_specs=[hbm] * 6 + [vmem] * 2 + [hbm, vmem] + [hbm] * 6 + [vmem] * 3,
        out_specs=(vmem,) * 6,
        scratch_shapes=[
            pltpu.VMEM(qa.shape, BF16),
            pltpu.VMEM(qa.shape, BF16),
            pltpu.VMEM(qa.shape, BF16),
            pltpu.VMEM(kt.shape, BF16),
            pltpu.VMEM(normed_t.shape, BF16),
            pltpu.VMEM((nh, SLOT, group), BF16),
            pltpu.VMEM((16, group), BF16),
            pltpu.VMEM((nh, cols, width), BF16),
            pltpu.VMEM((HDIM, group), F32),
            pltpu.VMEM((group, HDIM), F32),
            pltpu.VMEM((group, HDIM), F32),
            pltpu.VMEM((nh, group, cols), BF16),
            pltpu.VMEM((nt,) + chunked, BF16),
            pltpu.VMEM((2,) + chunked, BF16),
            pltpu.VMEM(chunked, BF16),
            pltpu.VMEM((nb, depth, cols), BF16),
            pltpu.VMEM((nb, depth, cols), BF16),
            pltpu.VMEM((nt, 8, width), F32),
            pltpu.VMEM((nt, 8, width), F32),
            small,
            pltpu.VMEM((nb, 8, width), F32),
            small,
            pltpu.SemaphoreType.DMA((sems,)),
            pltpu.SemaphoreType.DMA((sems,)),
            pltpu.SemaphoreType.DMA((spots,)),
        ]
        + bufs,
        compiler_params=pltpu.CompilerParams(
            collective_id=2, has_side_effects=True, vmem_limit_bytes=63 << 20
        ),
        cost_estimate=pl.CostEstimate(
            flops=4 * group * width * nh * cols, bytes_accessed=30 << 20, transcendentals=0
        ),
        name="back",
    )(qa, ka, va, kt, normed_t, grad, lse, x, mixed_grad, sm, *w3, *sources, *vecs)


def shape_kernel(hw, nh, f1_ref, f2_ref, f3_ref, gq_ref, wi_ref, wo_ref, wp_ref, q_ref, k_ref, v_ref):
    cut = f1_ref.shape[1]
    wi_ref[:, :cut] = f1_ref[...]
    wi_ref[:, cut:] = f3_ref[:, :SLOT]
    wo_ref[:, :cut] = f2_ref[...]
    wo_ref[:, cut:] = f3_ref[:, SLOT : 2 * SLOT]
    wp_ref[...] = f3_ref[:, 2 * SLOT :].T
    for c, ref in enumerate((q_ref, k_ref, v_ref)):
        ref[...] = jnp.concatenate(
            [gq_ref[h, :, c * HDIM : (c + 1) * HDIM] for h in range(nh)], 1
        )


def shape_outputs(f1, f2, f3, gq):
    depth, cut = f1.shape
    nh = gq.shape[0]
    hw = nh * HDIM
    fw = cut + SLOT
    vmem = pl.BlockSpec(memory_space=pltpu.VMEM)
    shape = jax.ShapeDtypeStruct
    return pl.pallas_call(
        functools.partial(shape_kernel, hw, nh),
        out_shape=(
            shape((depth, fw), F32),
            shape((depth, fw), F32),
            shape((hw, depth), F32),
            shape((depth, hw), F32),
            shape((depth, hw), F32),
            shape((depth, hw), F32),
        ),
        in_specs=[vmem] * 4,
        out_specs=(vmem,) * 6,
        name="shape_outputs",
    )(f1, f2, f3, gq)


def body(
    layer_input,
    doc_lengths,
    first_gain,
    first_shift,
    w_query,
    w_key,
    w_value,
    query_bias,
    value_bias,
    inner_gain,
    inner_shift,
    w_proj,
    proj_bias,
    second_gain,
    second_shift,
    w_in,
    in_bias,
    hidden_gain,
    hidden_shift,
    w_out,
    out_bias,
    cotangent,
):
    nt = lax.axis_size("tensor")
    nb = lax.axis_size("batch")
    rank = lax.axis_index("tensor")
    rows, width = layer_input.shape
    hw = w_query.shape[1]
    fw = w_in.shape[1]
    lengths = doc_lengths[0]

    pad = jnp.zeros((fw - 2 * hw,), BF16)
    row3 = jnp.concatenate([inner_gain, inner_shift, pad])
    row10 = jnp.concatenate([query_bias, value_bias, pad])
    vectors = [in_bias, hidden_gain, hidden_shift, row3, first_gain, first_shift, proj_bias]
    vectors += [second_gain, second_shift, out_bias, row10]
    sm = jnp.stack(vectors + [out_bias] * 5)
    w3 = (w_query.T, w_key.T, w_value.T)

    *slots, normed_t, heads, lse, wi_all, wo_all, wp_all, sm_all = front(
        lengths, layer_input, sm, *w3, w_in, w_out, w_proj, nt
    )
    layer_output, mixed_grad, heads_grad, s1, s2, s3, *vecs = middle(
        heads, layer_input, cotangent, (w_in, w_out, w_proj, sm),
        (wi_all, wo_all, wp_all, sm_all), ROWS, nt,
    )
    input_grad, f1, f2, f3, gq, e = back(
        slots, normed_t, heads_grad, lse, layer_input, mixed_grad, sm, w3, (s1, s2, s3), vecs,
        nt, nb,
    )
    g_in, g_out, g_proj, g_query, g_key, g_value = shape_outputs(f1, f2, f3, gq)

    place = lax.axis_index("batch") * nt + rank
    inner = e[:, 3, :].reshape(nt, 4, hw).transpose(1, 0, 2).reshape(4, width)
    narrow = jnp.concatenate([inner, e[:, 4, :], e[:2, 5, :]], 0)
    size = width // (nb * nt)
    narrow = lax.dynamic_slice(narrow, (0, place * size), (10, size))
    broad = e[:, 0:3, :].transpose(1, 0, 2).reshape(3, nt * fw)
    size = nt * fw // (nb * nt)
    broad = lax.dynamic_slice(broad, (0, place * size), (3, size))

    return (
        layer_output,
        input_grad,
        narrow[8],
        narrow[9],
        g_query,
        g_key,
        g_value,
        narrow[2],
        narrow[3],
        narrow[0],
        narrow[1],
        g_proj,
        narrow[4],
        narrow[5],
        narrow[6],
        g_in,
        broad[0],
        broad[1],
        broad[2],
        g_out.T,
        narrow[7],
    )


def solution(mesh):
    both = ("batch", "tensor")
    in_specs = (
        P(both, None),
        P("batch", None),
        P(),
        P(),
        P(None, "tensor"),
        P(None, "tensor"),
        P(None, "tensor"),
        P("tensor"),
        P("tensor"),
        P("tensor"),
        P("tensor"),
        P("tensor", None),
        P(),
        P(),
        P(),
        P(None, "tensor"),
        P("tensor"),
        P("tensor"),
        P("tensor"),
        P("tensor", None),
        P(),
        P(both, None),
    )
    vector = P(both)
    out_specs = (
        P(both, None),
        P(both, None),
        vector,
        vector,
        P("batch", "tensor"),
        P("batch", "tensor"),
        P("batch", "tensor"),
        vector,
        vector,
        vector,
        vector,
        P("tensor", "batch"),
        vector,
        vector,
        vector,
        P("batch", "tensor"),
        vector,
        vector,
        vector,
        P("tensor", "batch"),
        vector,
    )
    return jax.shard_map(body, mesh=mesh, in_specs=in_specs, out_specs=out_specs, check_vma=False)
```

```python
import functools
import math

import jax
import jax.numpy as jnp
from jax import lax
from jax.experimental import pallas as pl
from jax.experimental.pallas import tpu as pltpu
from jax.sharding import PartitionSpec as P

HDIM = 64
SLOT = 128
TILE = 512
LONGEST = 2048
EPS = 1e-05
SCALE = 0.125
LOG2E = 1.4426950408889634
NEG = -1e30
F32 = jnp.float32
BF16 = jnp.bfloat16


def dot_nn(a, b):
    return jnp.dot(a, b, preferred_element_type=F32)


def dot_nt(a, b):
    return lax.dot_general(a, b, (((1,), (1,)), ((), ())), preferred_element_type=F32)


def doc_ends(len_ref):
    ends = []
    total = jnp.int32(0)
    for i in range(len_ref.shape[0]):
        total = total + len_ref[i]
        ends.append(total)
    return ends


def halves_of(n):
    cut = next(i for i in range(1, n + 1) if 2 * i * (i + 1) >= n * (n + 1) - 2 * n)
    return [list(range(cut)), list(range(cut, n))]


def doc_lanes(len_ref, first, rows):
    ends = doc_ends(len_ref)
    lane = lax.broadcasted_iota(jnp.int32, (1, SLOT - HDIM), 1)
    low = jnp.zeros((1, SLOT - HDIM), jnp.int32)
    high = jnp.zeros((1, SLOT - HDIM), jnp.int32)
    for i, end in enumerate(ends):
        low = jnp.where(lane == i, end - len_ref[i], low)
        high = jnp.where(lane == i, end, high)
    pos = first + lax.broadcasted_iota(jnp.int32, (rows, 1), 0)
    return (pos >= low) & (pos < high)


def reaches(i, j):
    return (i - j) * TILE - (TILE - 1) < LONGEST


def causal(s):
    key = lax.broadcasted_iota(jnp.int32, s.shape, 0)
    query = lax.broadcasted_iota(jnp.int32, s.shape, 1)
    return jnp.where(key <= query, s, NEG)


def blk(i):
    return slice(i * TILE, (i + 1) * TILE)


def forward_tiles(h, blocks, qa_ref, ka_ref, vt_s, out_ref, lse_ref):
    at = slice(h * HDIM, (h + 1) * HDIM)
    for i in blocks:
        query = qa_ref[h, blk(i), :]
        peak = jnp.full((1, TILE), NEG, F32)
        acc = jnp.zeros((HDIM + 16, TILE), F32)
        for j in range(i + 1):
            if not reaches(i, j):
                continue
            s = dot_nt(ka_ref[h, blk(j), :], query)
            if i == j:
                s = causal(s)
            new = jnp.maximum(peak, jnp.max(s, 0, keepdims=True) * (SCALE * LOG2E))
            p = jnp.exp2(s * (SCALE * LOG2E) - new).astype(BF16)
            acc = acc * jnp.exp2(peak - new) + dot_nn(vt_s[h, : HDIM + 16, blk(j)], p)
            peak = new
        total = acc[HDIM : HDIM + 1]
        out_ref[at, blk(i)] = (acc[:HDIM] / total).astype(BF16)
        lse_ref[h : h + 1, blk(i)] = peak + jnp.log2(total)


MESH = pl.DeviceIdType.MESH
ROWS = 256


def flip1(i):
    return i + 1 - 2 * (i % 2)


def flip2(i):
    return i + 2 - 4 * ((i // 2) % 2)


def flips(t):
    return [t, flip1(t), flip2(t), flip1(flip2(t))]


def flip_bit(i, bit):
    return i + bit - 2 * bit * ((i // bit) % 2)


def greet(partners):
    barrier = pltpu.get_barrier_semaphore()
    for p in partners:
        pl.semaphore_signal(barrier, inc=1, device_id=p, device_id_type=MESH)
    pl.semaphore_wait(barrier, len(partners))


def copier(send, recv):
    def copy(src, dst, i, dev):
        return pltpu.make_async_remote_copy(
            src_ref=src,
            dst_ref=dst,
            send_sem=send.at[i],
            recv_sem=recv.at[i],
            device_id=dev,
            device_id_type=MESH,
        )

    return copy


def bits_of(n):
    return [1 << i for i in range(n.bit_length() - 1)]


def ln_stats(v, n):
    mean = jnp.sum(v, -1, keepdims=True) * (1.0 / n)
    var = jnp.sum(v * v, -1, keepdims=True) * (1.0 / n) - mean * mean
    return mean, lax.rsqrt(var + EPS)


def ln_back(dh, hat, inv, n):
    m0 = jnp.sum(dh, -1, keepdims=True) * (1.0 / n)
    m1 = jnp.sum(dh * hat, -1, keepdims=True) * (1.0 / n)
    return inv * (dh - m0 - hat * m1)


def col_sum(v):
    return jnp.sum(v, 0, keepdims=True)


def front_kernel(
    nh,
    len_ref, x_ref, wq_ref, wk_ref, wv_ref, wi_ref, wo_ref, wp_ref, *rest,
):
    vector_refs, rest = rest[:13], rest[13:]
    front_body(
        nh, len_ref, x_ref, wq_ref, wk_ref, wv_ref, wi_ref, wo_ref, wp_ref, vector_refs, *rest
    )


def front_body(
    nh,
    len_ref, x_ref, wq_ref, wk_ref, wv_ref, wi_ref, wo_ref, wp_ref, vector_refs,
    qa_ref, ka_ref, va_ref, kt_ref, nt_ref, out_ref, lse_ref, wi_all, wo_all, wp_all, sm_all, sm_ref,
    nrm, w_s, qa_s, ka_s, va_s, kt_s, nt_s, vt_s, send, recv, local,
):
    b = lax.axis_index("batch")
    t = lax.axis_index("tensor")
    ranks = flips(t)
    core, across = (b, ranks[1]), (b, ranks[2])
    side, near = (flip1(b), t), (flip2(b), t)
    rows, full_width = x_ref.shape
    chunks = rows // ROWS
    width = nh * HDIM
    copy = copier(send, recv)
    rows_of = [v[...].astype(F32).reshape(1, v.shape[0]) for v in vector_refs]
    qb, vb, ig, ins = rows_of[9:]
    pad = jnp.zeros((1, full_width - 2 * width), F32)
    rows_of[3:3] = [jnp.concatenate([ig, ins, pad], 1)]
    rows_of = rows_of[:10] + [jnp.concatenate([qb, vb, pad], 1), jnp.zeros((5, full_width), F32)]
    sm_ref[...] = jnp.concatenate(rows_of, 0).astype(BF16)
    greet([core, across, side, near])

    weights = [(wi_ref, wi_all), (wo_ref, wo_all), (wp_ref, wp_all)]
    order = [2, 0, 1]
    quarter = b % 4
    parts = [quarter, flip1(quarter), flip2(quarter), flip1(flip2(quarter))]

    def part(a, ref, q):
        depth = weights[a][0].shape[0] // 4
        return ref.at[pl.ds(pl.multiple_of(parts[q] * depth, depth), depth)]

    sends = []

    def go(c):
        c.start()
        sends.append(c)
        return c

    gain = sm_ref[4:5, :].astype(F32)
    shift = sm_ref[5:6, :].astype(F32)

    def chunk(j, k):
        return nrm.at[j, pl.ds(k * ROWS, ROWS)]

    near_by = []
    far = []
    for k in range(chunks):
        v = x_ref[k * ROWS : (k + 1) * ROWS, :].astype(F32)
        mean, inv = ln_stats(v, full_width)
        nrm[0, k * ROWS : (k + 1) * ROWS, :] = ((v - mean) * inv * gain + shift).astype(BF16)
        far.append(go(copy(chunk(0, k), chunk(2, k), 8 + chunks + k, across)))
        near_by.append(go(copy(chunk(0, k), chunk(1, k), 8 + k, core)))
    base = 8 + 3 * chunks
    whole = []
    for a in order:
        src, dst = weights[a]
        whole.append(go(copy(src, dst.at[0], 4 + a, core)))
    whole.append(go(copy(sm_ref, sm_all.at[0], 7, core)))

    for i, ref in enumerate((wq_ref, wk_ref, wv_ref)):
        w_s[i * width : (i + 1) * width, :] = ref[...]
    nt_s[full_width:, :] = jnp.ones((16, nt_s.shape[1]), BF16)
    biases = sm_ref[10:11, :].astype(F32)
    bias = jnp.concatenate(
        [biases[:, :width], jnp.zeros((1, width), F32), biases[:, width : 2 * width]], 1
    )
    lane = lax.broadcasted_iota(jnp.int32, (ROWS, SLOT - HDIM), 1)
    ones = jnp.where(lane < 16, 1.0, 0.0).astype(BF16)

    def project(j, k):
        first = pl.multiple_of(ranks[j] * rows + k * ROWS, ROWS)
        at = pl.ds(first, ROWS)
        low = nrm[j, k * ROWS : (k + 1) * ROWS, :]
        val = (dot_nt(low, w_s[...]) + bias).astype(BF16)
        nt_s[:full_width, at] = low.T
        inside = doc_lanes(len_ref, first, ROWS)
        member = inside.astype(F32).astype(BF16)
        outside = jnp.where(inside | (lane >= len_ref.shape[0]), 0.0, NEG).astype(BF16)
        for h in range(nh):
            q, k_, v = [val[:, c * width + h * HDIM : c * width + (h + 1) * HDIM] for c in range(3)]
            qa_s[h, at, :] = jnp.concatenate([q, outside], 1)
            keys = jnp.concatenate([k_, member], 1)
            ka_s[h, at, :] = keys
            kt_s[h, :, at] = keys.T[:HDIM]
            vals = jnp.concatenate([v, ones], 1)
            va_s[h, at, :] = vals
            vt_s[h, :, at] = vals.T[: HDIM + 16]

    def from_across(a):
        first[a].wait_recv()
        ref = part(a, weights[a][1].at[1], 0)
        go(copy(ref, ref, base + a, side))
        go(copy(ref, ref, base + 3 + a, near))
        to_core(a, 0)

    def to_core(a, q):
        ref = part(a, weights[a][1].at[1], q)
        go(copy(ref, part(a, weights[a][1].at[2], q), base + 9 + 4 * a + q, core))

    def from_sides(a):
        ref = part(a, weights[a][1].at[1], 1)
        copy(ref, ref, base + a, side).wait_recv()
        to_core(a, 1)
        ref = part(a, weights[a][1].at[1], 2)
        copy(ref, ref, base + 3 + a, near).wait_recv()
        to_core(a, 2)

    def from_across_last(a):
        last[a].wait_recv()
        to_core(a, 3)

    for k in range(chunks):
        project(0, k)
    for k in range(chunks):
        near_by[k].wait_recv()
        project(1, k)
    first, last = {}, {}
    for k in range(chunks):
        far[k].wait_recv()
        go(copy(chunk(2, k), chunk(3, k), 8 + 2 * chunks + k, core))
        if k == chunks - 1:
            small_x = go(copy(sm_ref, sm_all.at[1], 3, across))
            for a in order:
                src, dst = weights[a]
                first[a] = go(copy(part(a, src, 0), part(a, dst.at[1], 0), a, across))
            for a in order:
                src, dst = weights[a]
                last[a] = go(copy(part(a, src, 3), part(a, dst.at[1], 3), base + 6 + a, across))
        project(2, k)
    for k in range(chunks):
        copy(chunk(2, k), chunk(3, k), 8 + 2 * chunks + k, core).wait_recv()
        project(3, k)
    kept = [(qa_s, qa_ref), (ka_s, ka_ref), (va_s, va_ref), (kt_s, kt_ref), (nt_s, nt_ref)]
    stores = [pltpu.make_async_copy(s, d, local.at[i]) for i, (s, d) in enumerate(kept)]
    for c in stores:
        c.start()

    def small_on():
        small_x.wait_recv()
        go(copy(sm_all.at[1], sm_all.at[2], base + 21, core))

    steps = [
        [lambda: from_across(2), small_on],
        [lambda: from_across(0)],
        [lambda: from_across(1)],
        [lambda: from_sides(2), lambda: from_sides(0)],
        [lambda: from_sides(1), lambda: from_across_last(2)],
        [lambda: from_across_last(0), lambda: from_across_last(1)],
    ]
    for h in range(nh):
        for blocks in halves_of(qa_s.shape[1] // TILE):
            forward_tiles(h, blocks, qa_s, ka_s, vt_s, out_ref, lse_ref)
            if steps:
                for f in steps.pop(0):
                    f()
    for rest in steps:
        for f in rest:
            f()
    copy(sm_all.at[1], sm_all.at[2], base + 21, core).wait_recv()
    for c in whole:
        c.wait_recv()
    for a in order:
        for q in range(4):
            ref = part(a, weights[a][1].at[2], q)
            copy(ref, ref, base + 9 + 4 * a + q, core).wait_recv()
    for c in sends:
        c.wait_send()
    for c in stores:
        c.wait()


def front(lengths, x, vectors, wq, wk, wv, wi, wo, wp, nt):
    rows, width = x.shape
    group = rows * nt
    nh = wq.shape[0] // HDIM
    sems = 8 + 3 * (rows // ROWS) + 22
    vmem = pl.BlockSpec(memory_space=pltpu.VMEM)
    hbm = pl.BlockSpec(memory_space=pl.ANY)
    smem = pl.BlockSpec(memory_space=pltpu.SMEM)
    shape = jax.ShapeDtypeStruct
    slots = (nh, group, SLOT)
    return pl.pallas_call(
        functools.partial(front_kernel, nh),
        out_shape=(
            shape(slots, BF16),
            shape(slots, BF16),
            shape(slots, BF16),
            shape((nh, HDIM, group), BF16),
            shape((width + 16, group), BF16),
            shape((nh * HDIM, group), BF16),
            shape((nh, group), F32),
            shape((nt - 1,) + wi.shape, BF16),
            shape((nt - 1,) + wo.shape, BF16),
            shape((nt - 1,) + wp.shape, BF16),
            shape((nt - 1, 16, width), BF16),
            shape((16, width), BF16),
        ),
        in_specs=[smem] + [vmem] * 4 + [hbm] * 3 + [vmem] * 13,
        out_specs=(hbm,) * 5 + (vmem,) * 2 + (hbm,) * 4 + (vmem,),
        scratch_shapes=[
            pltpu.VMEM((nt, rows, width), BF16),
            pltpu.VMEM((3 * nh * HDIM, width), BF16),
            pltpu.VMEM(slots, BF16),
            pltpu.VMEM(slots, BF16),
            pltpu.VMEM(slots, BF16),
            pltpu.VMEM((nh, HDIM, group), BF16),
            pltpu.VMEM((width + 16, group), BF16),
            pltpu.VMEM((nh, HDIM + 16, group), BF16),
            pltpu.SemaphoreType.DMA((sems,)),
            pltpu.SemaphoreType.DMA((sems,)),
            pltpu.SemaphoreType.DMA((5,)),
        ],
        compiler_params=pltpu.CompilerParams(
            collective_id=0, has_side_effects=True, vmem_limit_bytes=56 << 20
        ),
        cost_estimate=pl.CostEstimate(
            flops=6 * group * width * nh * HDIM, bytes_accessed=20 << 20, transcendentals=0
        ),
        name="front",
    )(lengths, x, wq, wk, wv, wi, wo, wp, *vectors)


def mid_kernel(
    tm, nt,
    heads_ref, resid_ref, cot_ref, wi_own, wo_own, wp_own, wi_all, wo_all, wp_all,
    sm_own, sm_all,
    lout_ref, mg_ref, hg_all, o1_ref, o2_ref, o3_ref, vs_ref, is_ref, fs_ref,
    wi_s, wo_s, wp_s, hr_s, hg_s, act_s, dact_s, dh_s, hid_s, pre_s, inner_s,
    sec_t, cot_t, att_t, g1, g2, g3, r1, r2, r3, send, recv, local,
):
    b = lax.axis_index("batch")
    t = lax.axis_index("tensor")
    ranks = flips(t)
    devs = [(b, r) for r in ranks]
    step = pl.program_id(0)
    tiles = pl.num_programs(0) - nt
    n_tiles = hr_s.shape[2] // tm
    rows = n_tiles * tm
    width = resid_ref.shape[1]
    fw = wi_s.shape[2]
    ff = nt * fw
    hw = width // nt
    copy = copier(send, recv)

    def sm_row(j, i):
        ref = sm_own if j == 0 else sm_all.at[j - 1]
        return ref[i : i + 1, :].astype(F32)

    def lanes(rank, r):
        return pl.ds(pl.multiple_of(rank * rows + r * tm, tm), tm)

    def heads_in(j, r):
        return copy(
            heads_ref.at[:, lanes(ranks[j], r)],
            hr_s.at[j, :, pl.ds(pl.multiple_of(r * tm, tm), tm)],
            j * n_tiles + r,
            devs[j],
        )

    def own_heads():
        return pltpu.make_async_copy(
            heads_ref.at[:, pl.ds(pl.multiple_of(t * rows, tm), rows)], hr_s.at[0], local.at[6]
        )

    def grads_out(j, r):
        return copy(
            hg_s.at[j, :, pl.ds(pl.multiple_of(r * tm, tm), tm)],
            hg_all.at[:, lanes(t, r)],
            (nt + j) * n_tiles + r,
            devs[j],
        )

    def own_grads():
        return pltpu.make_async_copy(
            hg_s.at[0], hg_all.at[:, pl.ds(pl.multiple_of(t * rows, tm), rows)], local.at[7]
        )

    base = 2 * nt * n_tiles
    cut = g1.shape[2]

    given, taken, outs = [g1, g2, g3], [r1, r2, r3], [o1_ref, o2_ref, o3_ref]

    def pair_sum(i, s):
        return copy(given[i].at[s], taken[i].at[s], base + 2 * i + s, devs[1])

    def put(i, s):
        return pltpu.make_async_copy(taken[i].at[s], outs[i].at[s], local.at[2 * i + s])

    def loads(own, rest, dst, i):
        return [
            pltpu.make_async_copy(own, dst.at[0], local.at[8 + 2 * i]),
            pltpu.make_async_copy(rest, dst.at[pl.ds(1, nt - 1)], local.at[9 + 2 * i]),
        ]

    load_p = loads(wp_own, wp_all, wp_s, 0)
    load_i = loads(wi_own, wi_all, wi_s, 1)
    load_o = loads(wo_own, wo_all, wo_s, 2)

    @pl.when(step == 0)
    def _():
        for c in load_p + load_i + load_o:
            c.start()
        own_heads().start()
        greet(devs[1:])
        for r in range(n_tiles):
            for j in (2, 3, 1):
                heads_in(j, r).start()
        vs_ref[...] = jnp.zeros_like(vs_ref)
        is_ref[...] = jnp.zeros_like(is_ref)
        fs_ref[...] = jnp.zeros_like(fs_ref)
        for c in load_p:
            c.wait()
        own_heads().wait()

    @pl.when(step < tiles)
    def _():
        r0 = pl.multiple_of(step * tm, tm)
        here = pl.ds(r0, tm)
        for j in range(1, nt):
            heads_in(j, step).wait_recv()
        proj_bias, second_gain, second_shift, out_bias = [sm_row(0, i) for i in range(6, 10)]
        tails = [sm_row(j, 3) for j in range(nt)]
        inner_gain = jnp.concatenate([v[:, :hw] for v in tails], 1)
        inner_shift = jnp.concatenate([v[:, hw : 2 * hw] for v in tails], 1)
        heads_t = jnp.concatenate([hr_s[j, :, here] for j in range(nt)], 0)
        heads = heads_t.T.astype(F32)
        mean, inner_inv = ln_stats(heads, width)
        inner_hat = (heads - mean) * inner_inv
        inner_low = (inner_hat * inner_gain + inner_shift).astype(BF16)
        for j in range(nt):
            inner_s[j, here, :] = inner_low[:, j * hw : (j + 1) * hw]
        wp = jnp.concatenate([wp_s[j] for j in range(nt)], 0)
        mixed = resid_ref[...].astype(F32) + (dot_nn(inner_low, wp) + proj_bias)
        mean, second_inv = ln_stats(mixed, width)
        second_hat = (mixed - mean) * second_inv
        second_low = (second_hat * second_gain + second_shift).astype(BF16)
        sec_t[:, here] = second_low.T
        cot_low = cot_ref[...]
        cot_t[:, here] = cot_low.T
        cot = cot_low.astype(F32)

        @pl.when(step == 0)
        def _():
            for c in load_i:
                c.wait()

        c0 = math.sqrt(2.0 / math.pi)
        c1 = 0.044715
        s0 = jnp.zeros((tm, 1), F32)
        s1 = jnp.zeros((tm, 1), F32)
        for j in range(nt):
            v = dot_nn(second_low, wi_s[j]) + sm_row(j, 0)
            v2 = v * v
            th = jnp.tanh(v * (c0 + (c0 * c1) * v2))
            half = 0.5 + 0.5 * th
            act = v * half
            dact = half + (0.5 * v) * (1.0 - th * th) * (c0 + (3.0 * c0 * c1) * v2)
            act_s[j] = act
            dact_s[j] = dact
            s0 += jnp.sum(act, -1, keepdims=True)
            s1 += jnp.sum(act * act, -1, keepdims=True)
        mean = s0 * (1.0 / ff)
        inv = lax.rsqrt(s1 * (1.0 / ff) - mean * mean + EPS)
        result = mixed + out_bias
        m0 = jnp.zeros((tm, 1), F32)
        m1 = jnp.zeros((tm, 1), F32)

        @pl.when(step == 0)
        def _():
            for c in load_o:
                c.wait()

        for j in range(nt):
            gain = sm_row(j, 1)
            hat = (act_s[j] - mean) * inv
            act_s[j] = hat
            hid = (hat * gain + sm_row(j, 2)).astype(BF16)
            hid_s[j, here, :] = hid
            result += dot_nn(hid, wo_s[j])
            gh = dot_nt(cot_low, wo_s[j])
            gn = gh * hat
            fs_ref[j, 1:2, :] += col_sum(gn)
            fs_ref[j, 2:3, :] += col_sum(gh)
            dh = gh * gain
            dh_s[j] = dh
            m0 += jnp.sum(dh, -1, keepdims=True)
            m1 += jnp.sum(gn * gain, -1, keepdims=True)
        lout_ref[...] = result.astype(BF16)
        m0 = m0 * (1.0 / ff)
        m1 = m1 * (1.0 / ff)
        second_grad = jnp.zeros((tm, width), F32)
        for j in range(nt):
            pre = (inv * (dh_s[j] - m0 - act_s[j] * m1) * dact_s[j]).astype(BF16)
            pre_s[j, here, :] = pre
            fs_ref[j, 0:1, :] += col_sum(pre.astype(F32))
            second_grad += dot_nt(pre, wi_s[j])
        vs_ref[3:4, :] += col_sum(second_grad * second_hat)
        vs_ref[4:5, :] += col_sum(second_grad)
        vs_ref[5:6, :] += col_sum(cot)
        mixed_grad = cot + ln_back(second_grad * second_gain, second_hat, second_inv, width)
        mg_ref[...] = mixed_grad
        vs_ref[2:3, :] += col_sum(mixed_grad)
        att = mixed_grad.astype(BF16)
        att_t[:, here] = att.T
        grad_inner = dot_nt(att, wp)
        gain_sum = col_sum(grad_inner * inner_hat)
        shift_sum = col_sum(grad_inner)
        for j in range(nt):
            is_ref[j, 0:1, :] += gain_sum[:, j * hw : (j + 1) * hw]
            is_ref[j, 1:2, :] += shift_sum[:, j * hw : (j + 1) * hw]
        hg = ln_back(grad_inner * inner_gain, inner_hat, inner_inv, width).astype(BF16).T
        prod = hg.astype(F32) * heads_t.astype(F32)
        row = lax.broadcasted_iota(jnp.int32, (16, 1), 0)
        for j in range(nt):
            hg_s[j, :hw, here] = hg[j * hw : (j + 1) * hw, :]
            below = jnp.zeros((16, tm), F32)
            for h in range(hw // HDIM):
                delta = -col_sum(prod[j * hw + h * HDIM : j * hw + (h + 1) * HDIM, :])
                high = delta.astype(BF16).astype(F32)
                below = jnp.where(row == 2 * h, high, below)
                below = jnp.where(row == 2 * h + 1, delta - high, below)
            hg_s[j, hw:, here] = below.astype(BF16)
        for j in (2, 3, 1):
            grads_out(j, step).start()

    @pl.when(step == tiles)
    def _():
        own_grads().start()

    @pl.when((step >= tiles) & (step < tiles + 2))
    def _():
        s = step - tiles
        j = 2 * s + 1
        gi = dot_nn(sec_t[...], pre_s[j]).astype(BF16)
        g1[s] = gi[:, :cut]
        pair_sum(0, s).start()
        go = dot_nn(cot_t[...], hid_s[j]).astype(BF16)
        g2[s] = go[:, :cut]
        pair_sum(1, s).start()
        gp = dot_nn(att_t[...], inner_s[j]).astype(BF16)
        g3[s] = jnp.concatenate([gi[:, cut:], go[:, cut:], gp], 1)
        pair_sum(2, s).start()

    @pl.when(step >= tiles + 2)
    def _():
        s = step - tiles - 2
        j = 2 * s
        def add(i, mine):
            pair_sum(i, s).wait_recv()
            taken[i][s] = (mine + taken[i][s].astype(F32)).astype(BF16)
            put(i, s).start()

        gi = dot_nn(sec_t[...], pre_s[j])
        add(0, gi[:, :cut])
        go = dot_nn(cot_t[...], hid_s[j])
        add(1, go[:, :cut])
        gp = dot_nn(att_t[...], inner_s[j])
        add(2, jnp.concatenate([gi[:, cut:], go[:, cut:], gp], 1))

    @pl.when(step == pl.num_programs(0) - 1)
    def _():
        own_grads().wait()
        for r in range(n_tiles):
            for j in range(1, nt):
                heads_in(j, r).wait_send()
                grads_out(j, r).wait_send()
                grads_out(j, r).wait_recv()
        for i in range(3):
            for s in range(2):
                pair_sum(i, s).wait_send()
                put(i, s).wait()


def middle(heads, resid, cot, own, gathered, tm, nt):
    wi, wo, wp, sm = own
    hw, group = heads.shape
    rows, width = resid.shape
    fw = wi.shape[1]
    tiles = rows // tm
    last = tiles - 1
    tile = lambda i: jnp.minimum(i, last)
    hbm = pl.BlockSpec(memory_space=pl.ANY)
    vmem = pl.BlockSpec(memory_space=pltpu.VMEM)
    shape = jax.ShapeDtypeStruct
    block = pl.BlockSpec((tm, width), lambda i: (tile(i), 0))
    sems = 2 * nt * tiles + 6
    cut = fw - SLOT
    widths = [cut, cut, 2 * SLOT + hw]
    return pl.pallas_call(
        functools.partial(mid_kernel, tm, nt),
        out_shape=(
            shape((rows, width), BF16),
            shape((rows, width), F32),
            shape((hw + 16, group), BF16),
        )
        + tuple(shape((2, width, n), BF16) for n in widths)
        + (
            shape((8, width), F32),
            shape((nt, 8, hw), F32),
            shape((nt, 8, fw), F32),
        ),
        grid=(tiles + nt,),
        in_specs=[hbm, block, block] + [hbm] * 6 + [vmem] * 2,
        out_specs=(block, block) + (hbm,) * 4 + (vmem,) * 3,
        scratch_shapes=[
            pltpu.VMEM((nt,) + wi.shape, BF16),
            pltpu.VMEM((nt,) + wo.shape, BF16),
            pltpu.VMEM((nt,) + wp.shape, BF16),
            pltpu.VMEM((nt, hw, rows), BF16),
            pltpu.VMEM((nt, hw + 16, rows), BF16),
            pltpu.VMEM((nt, tm, fw), F32),
            pltpu.VMEM((nt, tm, fw), F32),
            pltpu.VMEM((nt, tm, fw), F32),
            pltpu.VMEM((nt, rows, fw), BF16),
            pltpu.VMEM((nt, rows, fw), BF16),
            pltpu.VMEM((nt, rows, hw), BF16),
            pltpu.VMEM((width, rows), BF16),
            pltpu.VMEM((width, rows), BF16),
            pltpu.VMEM((width, rows), BF16),
        ]
        + [pltpu.VMEM((2, width, n), BF16) for n in widths * 2]
        + [
            pltpu.SemaphoreType.DMA((sems,)),
            pltpu.SemaphoreType.DMA((sems,)),
            pltpu.SemaphoreType.DMA((14,)),
        ],
        compiler_params=pltpu.CompilerParams(
            collective_id=1, has_side_effects=True, vmem_limit_bytes=62 << 20
        ),
        cost_estimate=pl.CostEstimate(
            flops=12 * nt * rows * width * fw + 6 * rows * width * width,
            bytes_accessed=30 << 20,
            transcendentals=nt * rows * fw,
        ),
        name="middle",
    )(heads, resid, cot, wi, wo, wp, *gathered[:3], sm, gathered[3])


class Chain:
    def __init__(self, hops, source, came, kept, base, copy, local):
        self.hops, self.source, self.came, self.kept = hops, source, came, kept
        self.base, self.copy, self.local = base, copy, local
        self.at = 0

    def select(self, m, mine):
        kind, bit, _ = self.hops[m]
        buf = self.source if m == 0 else self.kept[m - 1]
        if kind == "x":
            return buf.at[pl.ds(0 if mine else 1, 1)]
        return buf.at[:, :, bit if mine else 1 - bit]

    def swap(self, m):
        return self.copy(self.select(m, False), self.came[m], self.base + m, self.hops[m][2])

    def loads(self):
        kind = self.hops[0][0]
        src = self.select(0, True)
        if kind != "b":
            return [pltpu.make_async_copy(src, self.kept[0], self.local.at[0])]
        return [
            pltpu.make_async_copy(src.at[:, i], self.kept[0].at[:, i // 2, i % 2], self.local.at[i])
            for i in range(src.shape[1])
        ]

    def start(self):
        self.swap(0).start()
        for c in self.loads():
            c.start()

    def advance(self):
        m = self.at
        self.at += 1
        kind = self.hops[m][0]
        last = m == len(self.hops) - 1
        self.swap(m).wait_recv()
        came = self.came[m]
        if m == 0:
            for c in self.loads():
                c.wait()
        if kind == "b":
            n = came.shape[1]
            for i in range(n):
                at = (slice(None), i // 2, i % 2) if n > 1 else (slice(None), 0, 0)
                if m == 0:
                    mine = self.kept[0][at]
                else:
                    mine = self.select(m, True)[:, i]
                total = mine.astype(F32) + came[:, i].astype(F32)
                if last:
                    return total
                self.kept[m][at] = total.astype(BF16)
        else:
            if m == 0:
                mine = self.kept[0][...]
            else:
                mine = self.select(m, True)[...]
            total = mine.astype(F32) + came[...].astype(F32)
            if last:
                return total[0, 0]
            self.kept[m][...] = total.astype(BF16)
        self.swap(m + 1).start()
        return None

    def finish(self):
        for m in range(len(self.hops)):
            self.swap(m).wait_send()


def chain_shapes(kinds, nb, rows, cols):
    wide = 2 if any(k[0] == "x" for k in kinds) else 1
    n = nb // 2
    tail = (rows, cols)
    source = (wide, n // 2, 2, 2) + tail if kinds[0][0] == "c" else (wide, n, 2) + tail
    came, kept = [], []
    for kind, _ in kinds:
        if kind == "c":
            n //= 2
            came.append((wide, n, 2) + tail)
            kept.append((wide, n, 2) + tail)
        elif kind == "x":
            wide = 1
            came.append((wide, n, 2) + tail)
            kept.append((wide, n, 2) + tail)
        else:
            came.append((wide, n) + tail)
            n //= 2
            kept.append((wide, max(n, 1), 2) + tail)
    return source, came, kept[:-1]


def group_list(n):
    left = list(range(n))
    groups = []
    while left:
        if len(groups) % 2 == 0:
            g = left.pop()
            groups.append((g, [(g, j) for j in left + [g] if reaches(g, j)]))
        else:
            g = left.pop(0)
            groups.append((g, [(i, g) for i in [g] + left if reaches(i, g)]))
    return groups


def chain_kinds(nb):
    bits = list(range(nb.bit_length() - 1))
    hops = [("b", i) for i in bits]
    x = [("x", None)]
    return [
        x + hops,
        hops[:2] + x + hops[2:],
        [("c", 1)] + x + hops[:1] + hops[2:],
    ]


def back_kernel(
    nt, nb, nh, kinds,
    qa_ref, ka_ref, va_ref, kt_ref, nt_ref, grad_ref, lse_ref, x_ref, mg_ref, sm_ref,
    wq_ref, wk_ref, wv_ref, s1_ref, s2_ref, s3_ref, vs_ref, is_ref, fs_ref,
    ig_ref, f1_ref, f2_ref, f3_ref, gq_ref, e_ref, l_ref,
    qa_s, ka_s, va_s, kt_s, nt_s, g_s, dl_s, wh_s, dq_s, dkv_s, d_s,
    part_s, core_r, far_r, q_s, q_r, q2_r, e_s, e1_r, sum1_s, e2_r, sum2_s, l_s, l2_r, l2_s,
    send, recv, local, *rest,
):
    b = lax.axis_index("batch")
    t = lax.axis_index("tensor")
    ranks = flips(t)
    core, across = (b, ranks[1]), (b, ranks[2])
    group = [(b, r) for r in ranks]
    everyone = [((b + i) % nb, t) for i in range(nb)]
    bits = bits_of(nb)
    chunks, _, width = x_ref.shape
    rows = chunks * ROWS
    total_rows = qa_s.shape[1]
    hw = nh * HDIM
    depth = width // nb
    copy = copier(send, recv)
    sems = [0]

    def take(n):
        sems[0] += n
        return sems[0] - n

    spots = [0]

    def fetch(src, dst):
        spots[0] += 1
        return pltpu.make_async_copy(src, dst, local.at[spots[0] - 1])

    load_head = []
    for h in range(nh):
        at = pl.ds(h * HDIM, HDIM)
        load_head.append(
            [fetch(r.at[h], s.at[h]) for r, s in ((qa_ref, qa_s), (ka_ref, ka_s), (va_ref, va_s), (kt_ref, kt_s))]
            + [fetch(grad_ref.at[at], g_s.at[h, pl.ds(0, HDIM)])]
        )
    load_delta = fetch(grad_ref.at[pl.ds(hw, 16)], dl_s)
    load_normed = fetch(nt_ref, nt_s)
    load_mixed = fetch(mg_ref, ig_ref)
    load_wh = [
        fetch(w.at[pl.ds(h * HDIM, HDIM)], wh_s.at[h, pl.ds(c * HDIM, HDIM)])
        for h in range(nh)
        for c, w in enumerate((wk_ref, wv_ref, wq_ref))
    ]
    for c in [load_delta] + load_head[0]:
        c.start()
    greet(group[1:] + everyone[1:])

    rest = list(rest)
    chains = []
    for i, kind in enumerate(kinds):
        source = [s1_ref, s2_ref, s3_ref][i]
        came = [rest.pop(0) for _ in kind]
        kept = [rest.pop(0) for _ in kind[1:]]
        hops = [
            ("x", None, across)
            if k == "x"
            else (k, (b // bits[bit]) % 2, (flip_bit(b, bits[bit]), t))
            for k, bit in kind
        ]
        n = nb // 2 if kind[0][0] == "b" else 1
        own = local.at[pl.ds(spots[0], n)]
        spots[0] += n
        chains.append(Chain(hops, source, came, kept, take(len(kind)), copy, own))
    def block_of(rank):
        return (rank + t) % 2 + 2 * ((rank // 2 + t // 2) % 2)

    nothing = jnp.zeros((1, width), F32)
    for r in range(nt):
        j = block_of(r)
        e_s[r, 0:3, :] = fs_ref[j, 0:3, :]
        inner = is_ref[j]
        e_s[r, 3:4, :] = jnp.concatenate([inner[0:1], inner[1:2], nothing[:, : 2 * hw]], 1)
        e_s[r, 4:5, :] = vs_ref[2 + r : 3 + r, :]
        e_s[r, 5:8, :] = jnp.zeros((3, width), F32)
    e_base = take(3 * nt + 2 * nb)

    def hop1(j):
        return copy(e_s.at[ranks[j]], e1_r.at[j], e_base + j, group[j])

    def hop2(i):
        return copy(sum1_s, e2_r.at[i], e_base + nt + i, everyone[i])

    def hop3(j, came=False):
        place = ranks[j] if came else t
        return copy(sum2_s, e_ref.at[place], e_base + nt + nb + j, group[j])

    def late1(i):
        return copy(l_s, l2_r.at[i], e_base + 2 * nt + nb + i, everyone[i])

    def late2(j, came=False):
        place = ranks[j] if came else t
        return copy(l2_s, l_ref.at[place], e_base + 2 * nt + 2 * nb + j, group[j])

    def vectors1():
        for j in range(1, nt):
            hop1(j).start()

    def vectors2():
        total = e_s[t]
        for j in range(1, nt):
            hop1(j).wait_recv()
            total += e1_r[j]
        sum1_s[...] = total
        for i in range(1, nb):
            hop2(i).start()

    def vectors3():
        total = sum1_s[...]
        for i in range(1, nb):
            hop2(i).wait_recv()
            total += e2_r[i]
        sum2_s[...] = total
        e_ref[t] = total
        for j in range(1, nt):
            hop3(j).start()

    vectors1()
    for c in chains:
        c.start()
    for loads in load_head[1:] + [[load_normed], load_wh, [load_mixed]]:
        for c in loads:
            c.start()
    row = lax.broadcasted_iota(jnp.int32, (16, 1), 0)
    load_delta.wait()
    for h in range(nh):
        delta = dl_s[2 * h : 2 * h + 2, :].astype(F32)
        below = jnp.where(row == 0, delta[0:1], jnp.where(row == 1, delta[1:2], 0.0))
        g_s[h, HDIM:, :] = below.astype(BF16)

    lane = lax.broadcasted_iota(jnp.int32, (1, SLOT), 1)
    first_lanes = lane < HDIM
    side_scale = jnp.where(first_lanes, SCALE, 1.0)

    def sides(h, i):
        query = qa_s[h, blk(i), :]
        plain = jnp.where(first_lanes, query, jnp.zeros_like(query))
        grad = g_s[h, :HDIM, blk(i)]
        return query, plain, jnp.concatenate([jnp.zeros_like(grad), grad], 0).T

    def tile(h, i, j, query, plain, grad):
        s = dot_nt(ka_s[h, blk(j), :], query)
        if i == j:
            s = causal(s)
        p = jnp.exp2(s * (SCALE * LOG2E) - lse_ref[h : h + 1, blk(i)])
        ds = (p * dot_nn(va_s[h, blk(j), : HDIM + 16], g_s[h, :, blk(i)])).astype(BF16)
        return (
            dot_nn(kt_s[h, :, blk(j)], ds),
            dot_nn(ds, plain) + dot_nn(p.astype(BF16), grad),
        )

    def run_group(h, g, pairs):
        if all(i == g for i, _ in pairs):
            three = sides(h, g)
            acc = dq_s[h, :, blk(g)]
            for i, j in pairs:
                dq, dkv = tile(h, i, j, *three)
                acc += dq
                dkv_s[h, blk(j), :] += dkv
            dq_s[h, :, blk(g)] = acc
        else:
            acc = dkv_s[h, blk(g), :]
            for i, j in pairs:
                dq, dkv = tile(h, i, j, *sides(h, i))
                dq_s[h, :, blk(i)] += dq
                acc += dkv
            dkv_s[h, blk(g), :] = acc
        d_s[h, blk(g), :SLOT] = (dkv_s[h, blk(g), :] * side_scale).astype(BF16)
        d_s[h, blk(g), SLOT:] = (dq_s[h, :, blk(g)] * SCALE).T.astype(BF16)

    dq_s[...] = jnp.zeros_like(dq_s)
    dkv_s[...] = jnp.zeros_like(dkv_s)
    depth = width // nb

    head_sums = []
    head_base = take(nh * (1 + nb // 2))
    low, high = b % 2, b // 2
    peers = [(((high + i) % (nb // 2)) * 2 + low, t) for i in range(nb // 2)]

    def pair_send(h):
        return copy(q_s.at[h, 1 - low], q_r.at[h], head_base + h, (flip_bit(b, 1), t))

    def peer_send(h, i):
        place = (high + i) % (nb // 2)
        return copy(q_s.at[h, low, place], q2_r.at[h, i], head_base + nh + h * (nb // 2) + i, peers[i])

    def weight_part(h):
        grad = dot_nn(nt_s[...], d_s[h])
        head_sums.append(grad[width : width + 1])
        grad = grad.astype(BF16)
        for i in range(nb):
            q_s[h, i % 2, i // 2] = grad[i * depth : (i + 1) * depth, :]
        pair_send(h).start()

    def weight_pair(h):
        pair_send(h).wait_recv()
        for i in range(nb // 2):
            q_s[h, low, i] = (q_s[h, low, i].astype(F32) + q_r[h, i].astype(F32)).astype(BF16)
        for i in range(1, nb // 2):
            peer_send(h, i).start()

    def weight_done(h):
        total = q_s[h, low, high].astype(F32)
        for i in range(1, nb // 2):
            peer_send(h, i).wait_recv()
            total += q2_r[h, i].astype(F32)
        gq_ref[h] = total

    core_base = take(2 * chunks)
    far_base = take(chunks)

    def to_core(kind, k):
        return copy(
            part_s.at[2 * kind + 1, k], core_r.at[kind, k], core_base + kind * chunks + k, core
        )

    def to_far(k):
        return copy(part_s.at[2, k], far_r.at[k], far_base + k, across)

    def give(c):
        rank, k = c // chunks, c % chunks
        at = slice(c * ROWS, (c + 1) * ROWS)
        part = dot_nn(d_s[0, at, :], wh_s[0])
        for h in range(1, nh):
            part += dot_nn(d_s[h, at, :], wh_s[h])
        j = block_of(rank)
        part_s[j, k] = part.astype(BF16)

        @pl.when(j == 1)
        def _():
            to_core(0, k).start()

        @pl.when(j == 3)
        def _():
            to_core(1, k).start()

    def relay(c):
        rank, k = c // chunks, c % chunks

        @pl.when(block_of(rank) == 2)
        def _():
            to_core(1, k).wait_recv()
            part_s[2, k] = (part_s[2, k].astype(F32) + core_r[1, k].astype(F32)).astype(BF16)
            to_far(k).start()

    outs = [f1_ref, f2_ref, f3_ref]

    def step(c):
        if c.at < len(c.hops):
            done = c.advance()
            if done is not None:
                outs[chains.index(c)][...] = done[0]

    groups = group_list(total_rows // TILE)
    per = TILE // ROWS
    joint = max(len(groups) - 2, 1)

    def chunks_of(g):
        return list(range(g * per, (g + 1) * per))

    pending = []
    for n, (g, pairs) in enumerate(groups[:joint]):
        for h in range(nh):
            if n == 0:
                for c in load_head[h]:
                    c.wait()
            run_group(h, g, pairs)
        if n == 0:
            for c in load_wh:
                c.wait()
            vectors2()
        if n == joint - 1:
            vectors3()
        for c in pending:
            relay(c)
        pending = chunks_of(g)
        for c in pending:
            give(c)
        if n > 0:
            for c in chains:
                step(c)
    load_normed.wait()
    for h in range(nh):
        for g, pairs in groups[joint:]:
            run_group(h, g, pairs)
        if h == 0:
            for c in pending:
                relay(c)
        if h == nh - 1:
            pending = sum([chunks_of(g) for g, _ in groups[joint:]], [])
            for c in pending:
                give(c)
            for c in pending:
                relay(c)
        weight_part(h)
        if h > 0:
            weight_pair(h - 1)

    gain = sm_ref[4:5, :].astype(F32)
    loads = [fetch(x_ref.at[k], part_s.at[3, k]) for k in range(chunks)]
    for k in range(chunks):
        to_core(1, k).wait_send()
        loads[k].start()
    firsts = [jnp.zeros((1, width), F32), jnp.zeros((1, width), F32)]
    load_mixed.wait()
    for k in range(chunks):
        to_core(0, k).wait_recv()
        to_far(k).wait_recv()
        grad = part_s[0, k].astype(F32) + core_r[0, k].astype(F32) + far_r[k].astype(F32)
        at = slice(k * ROWS, (k + 1) * ROWS)
        loads[k].wait()
        v = part_s[3, k].astype(F32)
        mean, inv = ln_stats(v, width)
        hat = (v - mean) * inv
        firsts[0] += col_sum(grad * hat)
        firsts[1] += col_sum(grad)
        ig_ref[at, :] += ln_back(grad * gain, hat, inv, width)
        if k == 0:
            weight_pair(nh - 1)

    sums = [s[:, 2 * HDIM :] for s in head_sums] + [s[:, HDIM : 2 * HDIM] for s in head_sums]
    half = width // 2
    for i in range(2):
        l_s[2 * i : 2 * i + 1, :] = firsts[i][:, :half]
        l_s[2 * i + 1 : 2 * i + 2, :] = firsts[i][:, half:]
    l_s[4:5, :] = jnp.concatenate(sums, 1)
    l_s[5:8, :] = jnp.zeros((3, half), F32)
    for i in range(1, nb):
        late1(i).start()
    turns = max(len(c.hops) for c in chains)
    for _ in range(turns):
        for c in chains:
            step(c)
    total = l_s[...]
    for i in range(1, nb):
        late1(i).wait_recv()
        total += l2_r[i]
    l2_s[...] = total
    l_ref[t] = total
    for j in range(1, nt):
        late2(j).start()
    for h in range(nh):
        weight_done(h)
    for k in range(chunks):
        to_core(0, k).wait_send()
        to_far(k).wait_send()
    for c in chains:
        c.finish()
    for h in range(nh):
        pair_send(h).wait_send()
        for i in range(1, nb // 2):
            peer_send(h, i).wait_send()
    for i in range(1, nb):
        hop2(i).wait_send()
        late1(i).wait_send()
    for j in range(1, nt):
        hop3(j, True).wait_recv()
        late2(j, True).wait_recv()
        hop1(j).wait_send()
        hop3(j).wait_send()
        late2(j).wait_send()


def back(slots, normed_t, grad, lse, x, mixed_grad, sm, w3, sums, vecs, nt, nb):
    qa, ka, va, kt = slots
    rows, width = x.shape
    nh, group, _ = qa.shape
    hw = nh * HDIM
    cols = 3 * HDIM
    depth = width // nb
    chunks = rows // ROWS
    kinds = chain_kinds(nb)
    widths = [s.shape[-1] for s in sums]
    bufs = []
    sources = []
    for i, kind in enumerate(kinds):
        source, came, kept = chain_shapes(kind, nb, depth, widths[i])
        sources.append(sums[i].reshape(source))
        bufs += [pltpu.VMEM(s, BF16) for s in came + kept]
    sems = sum(len(k) for k in kinds) + 3 * chunks + 2 * nb + 3 * nt + nh * (1 + nb // 2)
    spots = 5 * nh + 3 + 3 * nh + 2 + nb // 2 + chunks
    shape = jax.ShapeDtypeStruct
    vmem = pl.BlockSpec(memory_space=pltpu.VMEM)
    hbm = pl.BlockSpec(memory_space=pl.ANY)
    chunked = (chunks, ROWS, width)
    small = pltpu.VMEM((8, width), F32)
    return pl.pallas_call(
        functools.partial(back_kernel, nt, nb, nh, kinds),
        out_shape=(
            shape((rows, width), F32),
            shape((depth, widths[0]), F32),
            shape((depth, widths[1]), F32),
            shape((depth, widths[2]), F32),
            shape((nh, depth, cols), F32),
            shape((nt, 8, width), F32),
            shape((nt, 8, width // 2), F32),
        ),
        in_specs=[hbm] * 6 + [vmem] + [hbm] * 2 + [vmem] + [hbm] * 6 + [vmem] * 3,
        out_specs=(vmem,) * 7,
        scratch_shapes=[
            pltpu.VMEM(qa.shape, BF16),
            pltpu.VMEM(qa.shape, BF16),
            pltpu.VMEM(qa.shape, BF16),
            pltpu.VMEM(kt.shape, BF16),
            pltpu.VMEM(normed_t.shape, BF16),
            pltpu.VMEM((nh, HDIM + 16, group), BF16),
            pltpu.VMEM((16, group), BF16),
            pltpu.VMEM((nh, cols, width), BF16),
            pltpu.VMEM((nh, HDIM, group), F32),
            pltpu.VMEM((nh, group, SLOT), F32),
            pltpu.VMEM((nh, group, cols), BF16),
            pltpu.VMEM((nt,) + chunked, BF16),
            pltpu.VMEM((2,) + chunked, BF16),
            pltpu.VMEM(chunked, BF16),
            pltpu.VMEM((nh, 2, nb // 2, depth, cols), BF16),
            pltpu.VMEM((nh, nb // 2, depth, cols), BF16),
            pltpu.VMEM((nh, nb // 2, depth, cols), BF16),
            pltpu.VMEM((nt, 8, width), F32),
            pltpu.VMEM((nt, 8, width), F32),
            small,
            pltpu.VMEM((nb, 8, width), F32),
            small,
            pltpu.VMEM((8, width // 2), F32),
            pltpu.VMEM((nb, 8, width // 2), F32),
            pltpu.VMEM((8, width // 2), F32),
            pltpu.SemaphoreType.DMA((sems,)),
            pltpu.SemaphoreType.DMA((sems,)),
            pltpu.SemaphoreType.DMA((spots,)),
        ]
        + bufs,
        compiler_params=pltpu.CompilerParams(
            collective_id=2, has_side_effects=True, vmem_limit_bytes=63 << 20
        ),
        cost_estimate=pl.CostEstimate(
            flops=4 * group * width * nh * cols, bytes_accessed=30 << 20, transcendentals=0
        ),
        name="back",
    )(
        qa, ka, va, kt, normed_t, grad, lse, x.reshape(chunked), mixed_grad, sm, *w3, *sources, *vecs
    )


def shape_kernel(hw, nh, f1_ref, f2_ref, f3_ref, gq_ref, lo_ref, ig_ref, wi_ref, wo_ref, wp_ref, q_ref, k_ref, v_ref, lo_out, ig_out):
    lo_out[...] = lo_ref[...]
    ig_out[...] = ig_ref[...]
    cut = f1_ref.shape[1]
    wi_ref[:, :cut] = f1_ref[...]
    wi_ref[:, cut:] = f3_ref[:, :SLOT]
    wo_ref[:, :cut] = f2_ref[...]
    wo_ref[:, cut:] = f3_ref[:, SLOT : 2 * SLOT]
    wp_ref[...] = f3_ref[:, 2 * SLOT :].T
    for c, ref in enumerate((k_ref, v_ref, q_ref)):
        ref[...] = jnp.concatenate(
            [gq_ref[h, :, c * HDIM : (c + 1) * HDIM] for h in range(nh)], 1
        )


def shape_outputs(f1, f2, f3, gq, layer_output, input_grad):
    depth, cut = f1.shape
    nh = gq.shape[0]
    hw = nh * HDIM
    fw = cut + SLOT
    vmem = pl.BlockSpec(memory_space=pltpu.VMEM)
    shape = jax.ShapeDtypeStruct
    return pl.pallas_call(
        functools.partial(shape_kernel, hw, nh),
        out_shape=(
            shape((depth, fw), F32),
            shape((depth, fw), F32),
            shape((hw, depth), F32),
            shape((depth, hw), F32),
            shape((depth, hw), F32),
            shape((depth, hw), F32),
            shape(layer_output.shape, layer_output.dtype),
            shape(input_grad.shape, input_grad.dtype),
        ),
        in_specs=[vmem] * 6,
        out_specs=(vmem,) * 8,
        name="shape_outputs",
    )(f1, f2, f3, gq, layer_output, input_grad)


def body(
    layer_input,
    doc_lengths,
    first_gain,
    first_shift,
    w_query,
    w_key,
    w_value,
    query_bias,
    value_bias,
    inner_gain,
    inner_shift,
    w_proj,
    proj_bias,
    second_gain,
    second_shift,
    w_in,
    in_bias,
    hidden_gain,
    hidden_shift,
    w_out,
    out_bias,
    cotangent,
):
    nt = lax.axis_size("tensor")
    nb = lax.axis_size("batch")
    rank = lax.axis_index("tensor")
    rows, width = layer_input.shape
    hw = w_query.shape[1]
    fw = w_in.shape[1]
    lengths = doc_lengths[0]

    vectors = (in_bias, hidden_gain, hidden_shift, first_gain, first_shift, proj_bias)
    vectors += (second_gain, second_shift, out_bias)
    vectors += (query_bias, value_bias, inner_gain, inner_shift)
    w3 = (w_query.T, w_key.T, w_value.T)

    *slots, normed_t, heads, lse, wi_all, wo_all, wp_all, sm_all, sm = front(
        lengths, layer_input, vectors, *w3, w_in, w_out, w_proj, nt
    )
    layer_output, mixed_grad, heads_grad, s1, s2, s3, *vecs = middle(
        heads, layer_input, cotangent, (w_in, w_out, w_proj, sm),
        (wi_all, wo_all, wp_all, sm_all), ROWS, nt,
    )
    input_grad, f1, f2, f3, gq, e, late = back(
        slots, normed_t, heads_grad, lse, layer_input, mixed_grad, sm, w3, (s1, s2, s3), vecs,
        nt, nb,
    )
    g_in, g_out, g_proj, g_query, g_key, g_value, layer_output, input_grad = shape_outputs(
        f1, f2, f3, gq, layer_output, input_grad
    )

    place = lax.axis_index("batch") * nt + rank
    inner = e[:, 3, : 2 * hw].reshape(nt, 2, hw).transpose(1, 0, 2).reshape(2, width)
    ends = late[:, 4].reshape(nt, 2, hw).transpose(1, 0, 2).reshape(2, width)
    narrow = jnp.concatenate([inner, ends, e[:, 4, :], jnp.sum(late[:, :4], 0).reshape(2, width)], 0)
    size = width // (nb * nt)
    narrow = lax.dynamic_slice(narrow, (0, place * size), (10, size))
    broad = e[:, 0:3, :].transpose(1, 0, 2).reshape(3, nt * fw)
    size = nt * fw // (nb * nt)
    broad = lax.dynamic_slice(broad, (0, place * size), (3, size))

    return (
        layer_output,
        input_grad,
        narrow[8],
        narrow[9],
        g_query,
        g_key,
        g_value,
        narrow[2],
        narrow[3],
        narrow[0],
        narrow[1],
        g_proj,
        narrow[4],
        narrow[5],
        narrow[6],
        g_in,
        broad[0],
        broad[1],
        broad[2],
        g_out.T,
        narrow[7],
    )


def solution(mesh):
    both = ("batch", "tensor")
    in_specs = (
        P(both, None),
        P("batch", None),
        P(),
        P(),
        P(None, "tensor"),
        P(None, "tensor"),
        P(None, "tensor"),
        P("tensor"),
        P("tensor"),
        P("tensor"),
        P("tensor"),
        P("tensor", None),
        P(),
        P(),
        P(),
        P(None, "tensor"),
        P("tensor"),
        P("tensor"),
        P("tensor"),
        P("tensor", None),
        P(),
        P(both, None),
    )
    vector = P(both)
    out_specs = (
        P(both, None),
        P(both, None),
        vector,
        vector,
        P("batch", "tensor"),
        P("batch", "tensor"),
        P("batch", "tensor"),
        vector,
        vector,
        vector,
        vector,
        P("tensor", "batch"),
        vector,
        vector,
        vector,
        P("batch", "tensor"),
        vector,
        vector,
        vector,
        P("tensor", "batch"),
        vector,
    )
    return jax.shard_map(body, mesh=mesh, in_specs=in_specs, out_specs=out_specs, check_vma=False)
```
